256 devices in a mesh: grp: 8 (over z), dev: 32 (over x, y, core).
Axes of the slice: x: 4, y: 4, z: 8, core: 2. Of those that a mesh axis runs over, the one named last changes fastest.
Arguments:
- matrix: float32 [524288, 1024], P(('grp', 'dev')), may hold values from -60 to 60
- block_order: int32 [8, 512], P('grp'), may hold values from 0 to 511, as said below
- counts: int32 [8, 32], P('grp'), may hold values from 0 to 32, as said below
- sign_bits: int32 [8, 512, 128], P('grp'), may hold values from 0 to 1
- row_mask: int32 [8, 512, 128], P('grp'), may hold values from 0 to 1, as said below
Outputs:
- sketch: float32 [262144, 1024], P(('grp', 'dev'))
- group_factor: float32 [8, 1024, 1024], P('grp', 'dev')
- factor: float32 [1024, 1024], P('dev')
The draws below stay inside these ranges and needn't reach their ends.
Inputs may be any that keep to these rules, and one draw needn't show every extreme that they name: Each row of block_order is a permutation of the group's block indices; at most 1 block of one device's blocks are placed in the positions held by one device, and some pair reaches 1. `counts`: each row sums to 512; its largest entry is exactly 32. `row_mask`: exactly 32 ones in each row of 128.
All inputs are finite; a program needn't handle non-finite values.
Results may differ from the reference program's by a relative error of at most 0.0003.
Values sent between devices are 32-bit elements; how exact they have to be, the bound alone decides.
A program may use at most 128 MiB of HBM per device.

```python
import math
import jax
import jax.numpy as jnp
from jax import lax

COLS = 1024
BLOCK = 128
KEEP = 32
BLOCKS_DEV = 16
POSITIONS = 512
MOST = 32
ROWS = 524288
N_GRP = 8
N_DEV = 32


def layout_group(key):
    keys = jax.random.split(key, 5)
    positions = N_DEV * BLOCKS_DEV
    device_order = jax.random.permutation(keys[0], N_DEV).astype(jnp.int32)
    smaller = jax.random.randint(keys[1], (N_DEV // 2,), 0, BLOCKS_DEV + 1).astype(jnp.int32)
    smaller = smaller.at[0].set(0)
    count_row = jnp.zeros((N_DEV,), jnp.int32)
    count_row = count_row.at[device_order[0::2]].set(2 * BLOCKS_DEV - smaller)
    count_row = count_row.at[device_order[1::2]].set(smaller)
    run_ends = jnp.cumsum(count_row)
    block_locations = jnp.arange(positions, dtype=jnp.int32)
    owners = jnp.sum((block_locations[:, None] >= run_ends[None, :]).astype(jnp.int32), axis=1)
    relabel = jax.random.permutation(keys[2], N_DEV).astype(jnp.int32)
    source = relabel[block_locations % N_DEV]
    noise_one = jax.random.randint(keys[3], (positions,), 0, positions).astype(jnp.int32)
    within = jnp.argsort(owners * (positions * positions) + noise_one * positions + block_locations)
    source = source[within]
    noise_two = jax.random.randint(keys[4], (positions,), 0, positions).astype(jnp.int32)
    by_source = jnp.argsort(source * (positions * positions) + noise_two * positions + block_locations)
    ranks = jnp.zeros((positions,), jnp.int32).at[by_source].set(block_locations - source[by_source] * BLOCKS_DEV)
    return (source * BLOCKS_DEV + ranks, count_row)


def full_arrangement(key):
    group_keys = jax.random.split(jax.random.fold_in(key, 7), N_GRP)
    return jax.vmap(layout_group)(group_keys)


def draw_block_order(key, part):
    return full_arrangement(key)[0].astype(jnp.int32)


def draw_counts(key, part):
    return full_arrangement(key)[1].astype(jnp.int32)


def draw_row_mask(key, part):
    scores = jax.random.randint(key, (N_GRP, POSITIONS, BLOCK), 0, 2 ** 20).astype(jnp.int32)
    scores = scores * BLOCK + jnp.arange(BLOCK, dtype=jnp.int32)[None, None, :]
    ranks = jnp.argsort(jnp.argsort(scores, axis=2), axis=2)
    return (ranks < KEEP).astype(jnp.int32)


def draw_matrix(key, part):
    keys = jax.random.split(key, 3)
    col_scale = jnp.exp(jax.random.uniform(keys[2], (1, COLS), jnp.float32, math.log(0.3), math.log(3.0)))
    base = jnp.clip(jax.random.normal(keys[0], (ROWS, COLS), jnp.float32), -5.0, 5.0)
    row_scale = jnp.exp(jax.random.uniform(keys[1], (ROWS, 1), jnp.float32, math.log(0.3), math.log(3.0)))
    return (base * row_scale * col_scale).astype(jnp.float32)


def set_ends(array, rng, smallest, largest):
    longest = array.shape.index(max(array.shape))
    spots = []
    for shift in (0, 1):
        where = [jax.random.randint(jax.random.fold_in(rng, axis), (), 0, length) for axis, length in enumerate(array.shape)]
        where[longest] = (where[longest] + shift) % array.shape[longest]
        spots.append(tuple(where))
    return array.at[spots[0]].set(smallest).at[spots[1]].set(largest)


def setup_inputs(seed: int = 0) -> dict:
    streams_of = jax.random.split(jax.random.key(seed), 6)
    return {
        "matrix": draw_matrix(jax.random.fold_in(streams_of[5], 71), 0),
        "block_order": draw_block_order(jax.random.fold_in(streams_of[5], 71), 0),
        "counts": draw_counts(jax.random.fold_in(streams_of[5], 71), 0),
        "sign_bits": set_ends(jax.random.randint(streams_of[3], (N_GRP, POSITIONS, BLOCK), 0, 2), jax.random.fold_in(streams_of[3], 1), 0, 1).astype(jnp.int32),
        "row_mask": draw_row_mask(jax.random.fold_in(streams_of[5], 71), 0),
    }


def hadamard(order_of):
    indices = jnp.arange(order_of, dtype=jnp.int32)
    common = jnp.bitwise_and(indices[:, None], indices[None, :])
    parity = jnp.zeros_like(common)
    for shift_by in range(order_of.bit_length() - 1):
        parity = parity + jnp.bitwise_and(jnp.right_shift(common, shift_by), 1)
    return (1 - 2 * (parity % 2)).astype(jnp.float32)

def mix_blocks(block_list, mask_rows, sign_rows, walsh_sign_matrix):
    running = jnp.cumsum(mask_rows, axis=1) - 1
    choose_row = jnp.arange(KEEP, dtype=jnp.int32)[None, :, None]
    select_rows = ((mask_rows[:, None, :] == 1) & (running[:, None, :] == choose_row)).astype(jnp.float32)
    mixing_transform = jnp.einsum('jlf,fp->jlp', select_rows, walsh_sign_matrix, precision=lax.Precision.HIGHEST)
    mixing_transform = mixing_transform * (1 - 2 * sign_rows).astype(jnp.float32)[:, None, :]
    normalize_rows = float(walsh_sign_matrix.shape[0]) ** (-0.5)
    return jnp.einsum('uwd,udk->uwk', mixing_transform, block_list, precision=lax.Precision.HIGHEST) * normalize_rows

def reference(matrix, block_order, counts, sign_bits, row_mask):
    walsh_sign_matrix = hadamard(BLOCK)

    def one_group(group_id):
        group_rows = lax.dynamic_slice_in_dim(matrix, group_id * (POSITIONS * BLOCK), POSITIONS * BLOCK, 0)
        group_rows = group_rows.reshape(POSITIONS, BLOCK, COLS)
        order_row = lax.dynamic_index_in_dim(block_order, group_id, 0, False)
        count_row = lax.dynamic_index_in_dim(counts, group_id, 0, False)
        sign_rows = lax.dynamic_index_in_dim(sign_bits, group_id, 0, False)
        mask_rows = lax.dynamic_index_in_dim(row_mask, group_id, 0, False)
        picked = jnp.take(group_rows, order_row, axis=0)
        sketch_blocks = mix_blocks(picked, mask_rows, sign_rows, walsh_sign_matrix)
        flat_rows = sketch_blocks.reshape(POSITIONS * KEEP, COLS)
        group_gram = jnp.dot(flat_rows.T.astype(jnp.float32), flat_rows.astype(jnp.float32), precision=lax.Precision.HIGHEST, preferred_element_type=jnp.float32) / float(POSITIONS * KEEP)
        run_ends = jnp.cumsum(count_row)
        offsets = run_ends - count_row
        held_slots = jnp.arange(MOST, dtype=jnp.int32)
        slot_index = jnp.minimum(offsets[:, None] + held_slots[None, :], POSITIONS - 1).astype(jnp.int32)
        live_slot = held_slots[None, :] < count_row[:, None]
        sketch_output = jnp.take(sketch_blocks, slot_index.reshape(-1), axis=0).reshape(N_DEV, MOST, KEEP, COLS)
        sketch_output = jnp.where(live_slot[:, :, None, None], sketch_output, jnp.zeros_like(sketch_output))
        return (sketch_output, group_gram)
    sketch_all, group_grams = lax.map(one_group, jnp.arange(N_GRP, dtype=jnp.int32))
    lower_groups = jnp.linalg.cholesky(group_grams)
    group_factor = jnp.swapaxes(lower_groups, -1, -2)
    mean_gram = jnp.sum(group_grams, axis=0) / float(N_GRP)
    factor = jnp.linalg.cholesky(mean_gram).T
    return (sketch_all.reshape(N_GRP * N_DEV * MOST * KEEP, COLS), group_factor, factor)
```

```python
import jax
import jax.numpy as jnp
from jax import lax
from jax.experimental import pallas as pl
from jax.experimental.pallas import tpu as pltpu
from jax.sharding import PartitionSpec as P

MESH = pl.DeviceIdType.MESH
F32, BF16, I32 = jnp.float32, jnp.bfloat16, jnp.int32
BLOCK = 128
KEEP = 32
NB = 128
COLS = 1024
NBLK = COLS // NB
PER = 16
POSITIONS = 512
DEVS = 32
GRPS = 8
CHIPS = 16
SHARD = NBLK * (NBLK + 1) // 2 * NB // DEVS
ZROWS = 24


def packed(i, j):
    return i * NBLK - i * (i - 1) // 2 + (j - i)


def split2(x):
    h = x.astype(BF16)
    return h, (x - h.astype(F32)).astype(BF16)


def dot_t(a, b):
    return lax.dot_general(a, b, (((0,), (0,)), ((), ())), preferred_element_type=F32)


def dot_n(a, b):
    return lax.dot_general(a, b, (((1,), (0,)), ((), ())), preferred_element_type=F32)


def mix_kernel(order_in, counts_in, matrix, sign_bits, row_mask, send, gram, x, order, counts, signs, masks, s_rows, s_hi, s_mid, gram_v, place, tab_sem, in_sem, out_sem, gram_sem):
    me = lax.axis_index("dev")

    def fetch(k):
        return pltpu.make_async_copy(
            matrix.at[pl.ds(k * BLOCK, BLOCK)], x.at[pl.ds(k * BLOCK, BLOCK)], in_sem.at[k]
        )

    pairs = ((order_in, order), (counts_in, counts), (sign_bits, signs), (row_mask, masks))
    tables = [pltpu.make_async_copy(a, b, tab_sem.at[i]) for i, (a, b) in enumerate(pairs)]
    for table in tables:
        table.start()
    for k in range(PER):
        fetch(k).start()
    tables[0].wait()
    tables[1].wait()

    def find(p, carry):
        b = order[0, p]
        place[jnp.where((b >> 4) == me, b & 15, PER)] = p
        return carry

    lax.fori_loop(0, POSITIONS, find, 0, unroll=8)
    pos = [place[k] for k in range(PER)]

    def count(e, carry):
        run, owners = carry
        run = run + counts[0, e]
        return run, tuple(o + (p >= run).astype(I32) for o, p in zip(owners, pos))

    _, owners = lax.fori_loop(0, DEVS, count, (jnp.int32(0), (jnp.int32(0),) * PER))

    row = lax.broadcasted_iota(I32, (BLOCK, BLOCK), 0)
    col = lax.broadcasted_iota(I32, (BLOCK, BLOCK), 1)
    parity = row & col
    for shift in (4, 2, 1):
        parity = parity ^ (parity >> shift)
    walsh = (1 - 2 * (parity & 1)).astype(F32).astype(BF16)
    upto = jnp.where(row <= col, 1.0, 0.0).astype(BF16)
    tables[2].wait()
    tables[3].wait()
    mask = jnp.concatenate([masks[0, pl.ds(p, 1), :] for p in pos], axis=0).astype(F32)
    sign = jnp.concatenate([signs[0, pl.ds(p, 1), :] for p in pos], axis=0)
    sign = (1 - 2 * sign).astype(F32)
    running = dot_n(mask.astype(BF16), upto).astype(I32)
    nth = lax.broadcasted_iota(I32, (KEEP, BLOCK), 0) + 1
    chosen = [
        jnp.where((running[k : k + 1] == nth) & (mask[k : k + 1] > 0.5), 1.0, 0.0) for k in range(PER)
    ]
    mixing = dot_n(jnp.concatenate(chosen, axis=0).astype(BF16), walsh)

    outs = []
    for k in range(PER):
        t = (mixing[k * KEEP : (k + 1) * KEEP] * sign[k : k + 1]).astype(BF16)
        fetch(k).wait()
        block = x[k * BLOCK : (k + 1) * BLOCK, :]
        hi = block.astype(BF16)
        rest = block - hi.astype(F32)
        mid = rest.astype(BF16)
        low = (rest - mid.astype(F32)).astype(BF16)
        mixed = dot_n(t, hi) + dot_n(t, mid) + dot_n(t, low)
        mixed = mixed * float(BLOCK) ** -0.5
        rows = slice(k * KEEP, (k + 1) * KEEP)
        s_rows[rows, :] = mixed
        hi, mid = split2(mixed)
        s_hi[rows, :] = hi
        s_mid[rows, :] = mid
        out = pltpu.make_async_copy(s_rows.at[rows], send.at[owners[k]], out_sem.at[k])
        out.start()
        outs.append(out)

    for i in range(NBLK):
        a, b = i * NB, (i + 1) * NB
        block = dot_t(s_hi[:, a:b], s_hi[:, a:]) + dot_t(s_hi[:, a:b], s_mid[:, a:])
        block = block + dot_t(s_mid[:, a:b], s_hi[:, a:])
        for j in range(i, NBLK):
            at = packed(i, j) * NB
            gram_v[at : at + NB, :] = block[:, (j - i) * NB : (j - i + 1) * NB]
        rows = pl.ds(packed(i, i) * NB, (NBLK - i) * NB)
        out = pltpu.make_async_copy(gram_v.at[rows], gram.at[rows], gram_sem.at[i])
        out.start()
        outs.append(out)
    for out in outs:
        out.wait()


def mix(matrix, block_order, counts, sign_bits, row_mask):
    hbm = pl.BlockSpec(memory_space=pltpu.HBM)
    rows = PER * KEEP
    return pl.pallas_call(
        mix_kernel,
        out_shape=(
            jax.ShapeDtypeStruct((DEVS, KEEP, COLS), F32),
            jax.ShapeDtypeStruct((DEVS * SHARD, NB), F32),
        ),
        in_specs=[hbm] * 5,
        out_specs=(hbm, hbm),
        scratch_shapes=[
            pltpu.VMEM((PER * BLOCK, COLS), F32),
            pltpu.SMEM((1, POSITIONS), I32),
            pltpu.SMEM((1, DEVS), I32),
            pltpu.VMEM((1, POSITIONS, BLOCK), I32),
            pltpu.VMEM((1, POSITIONS, BLOCK), I32),
            pltpu.VMEM((rows, COLS), F32),
            pltpu.VMEM((rows, COLS), BF16),
            pltpu.VMEM((rows, COLS), BF16),
            pltpu.VMEM((DEVS * SHARD, NB), F32),
            pltpu.SMEM((PER + 1,), I32),
            pltpu.SemaphoreType.DMA((4,)),
            pltpu.SemaphoreType.DMA((PER,)),
            pltpu.SemaphoreType.DMA((PER,)),
            pltpu.SemaphoreType.DMA((NBLK,)),
        ],
        compiler_params=pltpu.CompilerParams(vmem_limit_bytes=62 << 20),
        name="mix_rows",
    )(block_order, counts, matrix, sign_bits, row_mask)


def reduce_kernel(g, full, mine, pair_buf, chip_buf, own, z_buf, z_sum, z_all, mean, own_sem, pair_sem, chip_sem, z_sem, m_sem, all_sem):
    grp = lax.axis_index("grp")
    dev = lax.axis_index("dev")
    core = lax.rem(dev, 2)
    chip = dev // 2
    cx, cy = chip // 4, lax.rem(chip, 4)

    def chip_at(d):
        return lax.rem(cx + d // 4, 4) * 4 + lax.rem(cy + lax.rem(d, 4), 4)

    def chip_back(d):
        return lax.rem(cx + 4 - d // 4, 4) * 4 + lax.rem(cy + 4 - lax.rem(d, 4), 4)

    def copy(src, dst, sem, at, to_grp, to_dev):
        return pltpu.make_async_remote_copy(
            src_ref=src,
            dst_ref=dst,
            send_sem=sem.at[(0, *at)],
            recv_sem=sem.at[(1, *at)],
            device_id=(to_grp, to_dev),
            device_id_type=MESH,
        )

    def z_start(z):
        return pl.multiple_of((z * 15) // 7 * 8, 8)

    partner = chip * 2 + 1 - core
    keep = pltpu.make_async_copy(g.at[core], mine, own_sem)
    keep.start()
    barrier = pltpu.get_barrier_semaphore()

    def greet(to_grp, to_dev):
        pl.semaphore_signal(barrier, inc=1, device_id=(to_grp, to_dev), device_id_type=MESH)

    greet(grp, partner)

    def greet_chip(d, c):
        greet(grp, chip_at(d) * 2)
        greet(grp, chip_at(d) * 2 + 1)
        return c

    def greet_z(d, c):
        greet(lax.rem(grp + d, GRPS), dev)
        return c

    lax.fori_loop(1, CHIPS, greet_chip, 0)
    lax.fori_loop(1, GRPS, greet_z, 0)
    pl.semaphore_wait(barrier, 1 + 2 * (CHIPS - 1) + GRPS - 1)

    pair = copy(g.at[1 - core], pair_buf, pair_sem, (), grp, partner)
    pair.start()
    keep.wait()
    pair.wait()

    def add_pair(i, c):
        pair_buf[i] = pair_buf[i] + mine[i]
        return c

    lax.fori_loop(0, CHIPS, add_pair, 0)

    def chip_copy(d):
        return copy(pair_buf.at[chip_at(d)], chip_buf.at[d], chip_sem, (d,), grp, chip_at(d) * 2 + core)

    def run(lo, hi, act):
        def step(d, c):
            act(d)
            return c

        lax.fori_loop(lo, hi, step, 0)

    run(1, CHIPS, lambda d: chip_copy(d).start())
    run(1, CHIPS, lambda d: chip_copy(d).wait())

    total = pair_buf[chip]
    for d in range(1, CHIPS):
        total = total + chip_buf[d]
    own[...] = total * (1.0 / (POSITIONS * KEEP))

    def z_copy(d):
        to = lax.rem(grp + d, GRPS)
        return copy(own.at[pl.ds(z_start(to), ZROWS)], z_buf.at[d], z_sem, (d,), to, dev)

    run(1, GRPS, lambda d: z_copy(d).start())

    def all_copy(src, d, to_core):
        return copy(src, full.at[core, chip], all_sem, (to_core, d), grp, chip_at(d) * 2 + to_core)

    def all_recv(c, d):
        return pltpu.make_async_remote_copy(
            src_ref=own,
            dst_ref=full.at[c, chip_back(d)],
            send_sem=all_sem.at[0, 0, d],
            recv_sem=rx_sem(c, d),
            device_id=(grp, partner),
            device_id_type=MESH,
        )

    def rx_sem(c, d):
        return all_sem.at[1, c, d]

    def gather_copy(src, d, to_core):
        return pltpu.make_async_remote_copy(
            src_ref=src,
            dst_ref=full.at[core, chip],
            send_sem=all_sem.at[0, to_core, d],
            recv_sem=rx_sem(core, d),
            device_id=(grp, chip_at(d) * 2 + to_core),
            device_id_type=MESH,
        )

    run(1, CHIPS, lambda d: gather_copy(own, d, 0).start())

    @pl.when(core == 1)
    def _():
        gather_copy(own, 0, 0).start()

    @pl.when(core == 0)
    def _():
        full[0, chip] = own[...]

    run(1, GRPS, lambda d: z_copy(d).wait())
    total = own[pl.ds(z_start(grp), ZROWS), :]
    for d in range(1, GRPS):
        total = total + z_buf[d]
    z_sum[...] = total * (1.0 / GRPS)

    def m_copy(d):
        return copy(z_sum, z_all.at[grp], m_sem, (d,), lax.rem(grp + d, GRPS), dev)

    run(1, GRPS, lambda d: m_copy(d).start())
    z_all[grp] = z_sum[...]

    def m_recv(d):
        return copy(z_sum, z_all.at[lax.rem(grp + GRPS - d, GRPS)], m_sem, (d,), grp, partner)

    run(1, GRPS, lambda d: m_recv(d).wait_recv())
    run(1, GRPS, lambda d: m_copy(d).wait_send())
    for z in range(GRPS):
        at = (z * 15) // 7 * 8
        mean[at : at + ZROWS, :] = z_all[z]

    run(1, CHIPS, lambda d: gather_copy(mean, d, 1).start())

    @pl.when(core == 0)
    def _():
        gather_copy(mean, 0, 1).start()

    @pl.when(core == 1)
    def _():
        full[1, chip] = mean[...]

    def finish(d):
        all_recv(0, d).wait_recv()
        all_recv(1, d).wait_recv()
        gather_copy(own, d, 0).wait_send()
        gather_copy(mean, d, 1).wait_send()

    run(1, CHIPS, finish)

    @pl.when(core == 1)
    def _():
        all_recv(0, 0).wait_recv()
        gather_copy(own, 0, 0).wait_send()

    @pl.when(core == 0)
    def _():
        all_recv(1, 0).wait_recv()
        gather_copy(mean, 0, 1).wait_send()


def reduce_gram(gram):
    vmem = pl.BlockSpec(memory_space=pltpu.VMEM)
    dma = pltpu.SemaphoreType.DMA
    return pl.pallas_call(
        reduce_kernel,
        out_shape=jax.ShapeDtypeStruct((2, CHIPS, SHARD, NB), F32),
        in_specs=[pl.BlockSpec(memory_space=pltpu.HBM)],
        out_specs=vmem,
        scratch_shapes=[
            pltpu.VMEM((CHIPS, SHARD, NB), F32),
            pltpu.VMEM((CHIPS, SHARD, NB), F32),
            pltpu.VMEM((CHIPS, SHARD, NB), F32),
            pltpu.VMEM((SHARD, NB), F32),
            pltpu.VMEM((GRPS, ZROWS, NB), F32),
            pltpu.VMEM((ZROWS, NB), F32),
            pltpu.VMEM((GRPS, ZROWS, NB), F32),
            pltpu.VMEM((SHARD, NB), F32),
            dma,
            dma((2,)),
            dma((2, CHIPS)),
            dma((2, GRPS)),
            dma((2, GRPS)),
            dma((2, 2, CHIPS)),
        ],
        compiler_params=pltpu.CompilerParams(
            collective_id=0, has_side_effects=True, vmem_limit_bytes=61 << 20
        ),
        name="reduce_gram",
    )(gram.reshape(2, CHIPS, SHARD, NB))


def diag_factor(d):
    n = NB // 8
    lane = lax.broadcasted_iota(I32, (8, NB), 1)
    sub = lax.broadcasted_iota(I32, (8, NB), 0)
    t_rows = [d[8 * s : 8 * s + 8, :] for s in range(n)]
    e_rows = [jnp.where(lane == sub + 8 * s, 1.0, 0.0).astype(F32) for s in range(n)]
    r_out, e_out = [], []
    for s in range(n):
        c0 = 8 * s
        t, e = t_rows[s], e_rows[s]
        cols = [jnp.broadcast_to(t[:, c0 + j : c0 + j + 1], (8, NB)) for j in range(8)]
        b = {}
        for i in range(8):
            for j in range(i, 8):
                b[i, j] = jnp.broadcast_to(cols[j][i : i + 1, :], (8, NB))
        rows = [jnp.broadcast_to(t[j : j + 1, :], (8, NB)) for j in range(8)]
        extra = [jnp.broadcast_to(e[j : j + 1, :], (8, NB)) for j in range(8)]
        r_strip = e_strip = None
        for j in range(8):
            scale = lax.rsqrt(b[j, j])
            low = {k: b[j, k] * scale for k in range(j + 1, 8)}
            for i in range(j + 1, 8):
                for k in range(i, 8):
                    b[i, k] = b[i, k] - low[i] * low[k]
            rj, ej = rows[j] * scale, extra[j] * scale
            for i in range(j + 1, 8):
                rows[i] = rows[i] - low[i] * rj
                extra[i] = extra[i] - low[i] * ej
            r_strip = rj if j == 0 else jnp.where(sub == j, rj, r_strip)
            e_strip = ej if j == 0 else jnp.where(sub == j, ej, e_strip)
        r_out.append(r_strip)
        e_out.append(e_strip)
        if s == n - 1:
            break
        w = jnp.concatenate([r_strip, e_strip], axis=1)
        h = w.astype(BF16).astype(F32)
        rest = w - h
        m = rest.astype(BF16).astype(F32)
        q = rest - m
        lhs = jnp.concatenate([v[:, :NB] for v in (h, h, m, m, h, q)], axis=0).astype(BF16)
        rhs = jnp.concatenate([h, m, h, m, q, h], axis=0).astype(BF16)
        update = dot_t(lhs, rhs)
        for i in range(s + 1, n):
            t_rows[i] = t_rows[i] - update[8 * i : 8 * i + 8, :NB]
            e_rows[i] = e_rows[i] - update[8 * i : 8 * i + 8, NB:]
    return jnp.concatenate(r_out, axis=0), jnp.concatenate(e_out, axis=0)


def cholesky_kernel(g, out, a, r, d):
    for i in range(NBLK):
        for j in range(i, NBLK):
            at = packed(i, j) * NB
            a[i * NB : (i + 1) * NB, j * NB : (j + 1) * NB] = g[at : at + NB, :]
    row = lax.broadcasted_iota(I32, (NB, NB), 0)
    col = lax.broadcasted_iota(I32, (NB, NB), 1)
    d[...] = a[0:NB, 0:NB]

    def step(k, c):
        top, inverse = diag_factor(d[...])
        d[...] = jnp.where(row <= col, top, 0.0)
        hi, mid = split2(inverse)
        left = jnp.concatenate([hi, hi, mid], axis=1)
        for kk in range(NBLK):

            @pl.when(k == kk)
            def _():
                k0, k1 = kk * NB, (kk + 1) * NB
                r[k0:k1, k0:k1] = d[...]
                if kk:
                    r[k0:k1, 0:k0] = jnp.zeros((NB, k0), F32)
                if kk == NBLK - 1:
                    return
                hi, mid = split2(a[k0:k1, k1:])
                strip = dot_n(left, jnp.concatenate([hi, mid, hi], axis=0))
                r[k0:k1, k1:] = strip
                hi, mid = split2(strip)
                lhs = jnp.concatenate([hi, hi, mid], axis=0)
                rhs = jnp.concatenate([hi, mid, hi], axis=0)
                d[...] = a[k1 : k1 + NB, k1 : k1 + NB] - dot_t(lhs[:, :NB], rhs[:, :NB])
                for i in range((COLS - k1) // NB):
                    lo, hi_ = i * NB, (i + 1) * NB
                    if i:
                        a[k1 + lo : k1 + hi_, k1 + lo :] -= dot_t(lhs[:, lo:hi_], rhs[:, lo:])
                    elif kk < NBLK - 2:
                        a[k1 : k1 + NB, k1 + NB :] -= dot_t(lhs[:, :NB], rhs[:, NB:])

        return c

    lax.fori_loop(0, NBLK, step, 0)
    chip = lax.axis_index("dev") // 2
    out[...] = r[pl.ds(pl.multiple_of(chip * 64, 64), 64), :]


def cholesky_rows(full):
    vmem = pl.BlockSpec(memory_space=pltpu.VMEM)
    return pl.pallas_call(
        cholesky_kernel,
        out_shape=jax.ShapeDtypeStruct((2 * COLS // DEVS, COLS), F32),
        in_specs=[vmem],
        out_specs=vmem,
        scratch_shapes=[
            pltpu.VMEM((COLS, COLS), F32),
            pltpu.VMEM((COLS, COLS), F32),
            pltpu.VMEM((NB, NB), F32),
        ],
        compiler_params=pltpu.CompilerParams(vmem_limit_bytes=32 << 20),
        cost_estimate=pl.CostEstimate(flops=50_000_000_000, bytes_accessed=100_000_000, transcendentals=0),
        name="cholesky_rows",
    )(full.reshape(DEVS * SHARD, NB))


def place_kernel(order_in, counts_in, arrived, sketch, order, counts, stage, zero, tab_sem, in_sem, sem):
    me = lax.axis_index("dev")
    tables = [
        pltpu.make_async_copy(order_in, order, tab_sem.at[0]),
        pltpu.make_async_copy(counts_in, counts, tab_sem.at[1]),
    ]
    for table in tables:
        table.start()
    zero[...] = jnp.zeros_like(zero)
    for table in tables:
        table.wait()

    def add(e, c):
        return c + jnp.where(e < me, counts[0, e], 0)

    offset = lax.fori_loop(0, DEVS, add, jnp.int32(0))
    held = counts[0, me]

    def load(j):
        source = order[0, jnp.minimum(offset + j, POSITIONS - 1)] >> 4
        return pltpu.make_async_copy(arrived.at[source], stage.at[j], in_sem.at[j])

    def start(j, c):
        @pl.when(j < held)
        def _():
            load(j).start()

        @pl.when(j >= held)
        def _():
            pltpu.make_async_copy(zero, sketch.at[j], sem.at[j]).start()

        return c

    def store(j, c):
        @pl.when(j < held)
        def _():
            load(j).wait()
            pltpu.make_async_copy(stage.at[j], sketch.at[j], sem.at[j]).start()

        return c

    def wait(j, c):
        pltpu.make_async_copy(zero, sketch.at[j], sem.at[j]).wait()
        return c

    lax.fori_loop(0, DEVS, start, 0)
    lax.fori_loop(0, DEVS, store, 0)
    lax.fori_loop(0, DEVS, wait, 0)


def place(block_order, counts, arrived):
    hbm = pl.BlockSpec(memory_space=pltpu.HBM)
    return pl.pallas_call(
        place_kernel,
        out_shape=jax.ShapeDtypeStruct((DEVS, KEEP, COLS), F32),
        in_specs=[hbm] * 3,
        out_specs=hbm,
        scratch_shapes=[
            pltpu.SMEM((1, POSITIONS), I32),
            pltpu.SMEM((1, DEVS), I32),
            pltpu.VMEM((DEVS, KEEP, COLS), F32),
            pltpu.VMEM((KEEP, COLS), F32),
            pltpu.SemaphoreType.DMA((2,)),
            pltpu.SemaphoreType.DMA((DEVS,)),
            pltpu.SemaphoreType.DMA((DEVS,)),
        ],
        compiler_params=pltpu.CompilerParams(vmem_limit_bytes=16 << 20),
        name="place_slots",
    )(block_order, counts, arrived)


def body(matrix, block_order, counts, sign_bits, row_mask):
    send, gram = mix(matrix, block_order, counts, sign_bits, row_mask)
    full = reduce_gram(gram)
    send, full = lax.optimization_barrier((send, full))
    arrived = lax.all_to_all(send, "dev", split_axis=0, concat_axis=0, tiled=True)
    rows = cholesky_rows(full)
    half = rows.shape[0] // 2
    first = lax.rem(lax.axis_index("dev"), 2) == 0
    mine = jnp.where(first, rows[:half], rows[half:])
    other = jnp.where(first, rows[half:], rows[:half])
    other = lax.ppermute(other, "dev", [(d, d ^ 1) for d in range(DEVS)])
    sketch = place(block_order, counts, arrived)
    group_factor = jnp.where(first, mine, other)[None]
    factor = jnp.where(first, other, mine)
    return sketch.reshape(DEVS * KEEP, COLS), group_factor, factor


def solution(mesh):
    placed = (
        P(("grp", "dev"), None),
        P("grp", None),
        P("grp", None),
        P("grp", None, None),
        P("grp", None, None),
    )
    return jax.shard_map(
        body,
        mesh=mesh,
        in_specs=placed,
        out_specs=(P(("grp", "dev"), None), P("grp", "dev", None), P("dev", None)),
        check_vma=False,
    )
```

```python
import jax
import jax.numpy as jnp
from jax import lax
from jax.experimental import pallas as pl
from jax.experimental.pallas import tpu as pltpu
from jax.sharding import PartitionSpec as P

MESH = pl.DeviceIdType.MESH
F32, BF16, I32 = jnp.float32, jnp.bfloat16, jnp.int32
BLOCK = 128
KEEP = 32
NB = 128
COLS = 1024
NBLK = COLS // NB
PER = 16
POSITIONS = 512
DEVS = 32
GRPS = 8
CHIPS = 16
SHARD = NBLK * (NBLK + 1) // 2 * NB // DEVS
ZROWS = 24
HALF = SHARD // 2
CUT = 40


def packed(i, j):
    return i * NBLK - i * (i - 1) // 2 + (j - i)


def split2(x):
    h = x.astype(BF16)
    return h, (x - h.astype(F32)).astype(BF16)


def dot_t(a, b):
    return lax.dot_general(a, b, (((0,), (0,)), ((), ())), preferred_element_type=F32)


def dot_n(a, b):
    return lax.dot_general(a, b, (((1,), (0,)), ((), ())), preferred_element_type=F32)


def mix_kernel(order_in, counts_in, matrix, sign_bits, row_mask, send, gram, x, order, counts, signs, masks, s_rows, s_hi, s_mid, gram_v, place, tab_sem, in_sem, out_sem, gram_sem):
    me = lax.axis_index("dev")

    def fetch(k):
        return pltpu.make_async_copy(
            matrix.at[pl.ds(k * BLOCK, BLOCK)], x.at[pl.ds(k * BLOCK, BLOCK)], in_sem.at[k]
        )

    pairs = ((order_in, order), (counts_in, counts), (sign_bits, signs), (row_mask, masks))
    tables = [pltpu.make_async_copy(a, b, tab_sem.at[i]) for i, (a, b) in enumerate(pairs)]
    for table in tables:
        table.start()
    for k in range(PER):
        fetch(k).start()
    tables[0].wait()
    tables[1].wait()

    def find(p, carry):
        b = order[0, p]
        place[jnp.where((b >> 4) == me, b & 15, PER)] = p
        return carry

    lax.fori_loop(0, POSITIONS, find, 0, unroll=8)
    pos = [place[k] for k in range(PER)]

    def count(e, carry):
        run, owners = carry
        run = run + counts[0, e]
        return run, tuple(o + (p >= run).astype(I32) for o, p in zip(owners, pos))

    _, owners = lax.fori_loop(0, DEVS, count, (jnp.int32(0), (jnp.int32(0),) * PER))

    row = lax.broadcasted_iota(I32, (BLOCK, BLOCK), 0)
    col = lax.broadcasted_iota(I32, (BLOCK, BLOCK), 1)
    parity = row & col
    for shift in (4, 2, 1):
        parity = parity ^ (parity >> shift)
    walsh = (1 - 2 * (parity & 1)).astype(F32).astype(BF16)
    upto = jnp.where(row <= col, 1.0, 0.0).astype(BF16)
    tables[2].wait()
    tables[3].wait()
    mask = jnp.concatenate([masks[0, pl.ds(p, 1), :] for p in pos], axis=0).astype(F32)
    sign = jnp.concatenate([signs[0, pl.ds(p, 1), :] for p in pos], axis=0)
    sign = (1 - 2 * sign).astype(F32)
    running = dot_n(mask.astype(BF16), upto).astype(I32)
    nth = lax.broadcasted_iota(I32, (KEEP, BLOCK), 0) + 1
    chosen = [
        jnp.where((running[k : k + 1] == nth) & (mask[k : k + 1] > 0.5), 1.0, 0.0) for k in range(PER)
    ]
    mixing = dot_n(jnp.concatenate(chosen, axis=0).astype(BF16), walsh)

    outs = []
    for k in range(PER):
        t = (mixing[k * KEEP : (k + 1) * KEEP] * sign[k : k + 1]).astype(BF16)
        fetch(k).wait()
        block = x[k * BLOCK : (k + 1) * BLOCK, :]
        hi = block.astype(BF16)
        rest = block - hi.astype(F32)
        mid = rest.astype(BF16)
        low = (rest - mid.astype(F32)).astype(BF16)
        mixed = dot_n(t, hi) + dot_n(t, mid) + dot_n(t, low)
        mixed = mixed * float(BLOCK) ** -0.5
        rows = slice(k * KEEP, (k + 1) * KEEP)
        s_rows[rows, :] = mixed
        hi, mid = split2(mixed)
        s_hi[rows, :] = hi
        s_mid[rows, :] = mid
        out = pltpu.make_async_copy(s_rows.at[rows], send.at[owners[k]], out_sem.at[k])
        out.start()
        outs.append(out)

    for i in range(NBLK):
        a, b = i * NB, (i + 1) * NB
        block = dot_t(s_hi[:, a:b], s_hi[:, a:]) + dot_t(s_hi[:, a:b], s_mid[:, a:])
        block = block + dot_t(s_mid[:, a:b], s_hi[:, a:])
        for j in range(i, NBLK):
            at = packed(i, j) * NB
            gram_v[at : at + NB, :] = block[:, (j - i) * NB : (j - i + 1) * NB]
        rows = pl.ds(packed(i, i) * NB, (NBLK - i) * NB)
        out = pltpu.make_async_copy(gram_v.at[rows], gram.at[rows], gram_sem.at[i])
        out.start()
        outs.append(out)
    for out in outs:
        out.wait()


def mix(matrix, block_order, counts, sign_bits, row_mask):
    hbm = pl.BlockSpec(memory_space=pltpu.HBM)
    rows = PER * KEEP
    return pl.pallas_call(
        mix_kernel,
        out_shape=(
            jax.ShapeDtypeStruct((DEVS, KEEP, COLS), F32),
            jax.ShapeDtypeStruct((DEVS * SHARD, NB), F32),
        ),
        in_specs=[hbm] * 5,
        out_specs=(hbm, hbm),
        scratch_shapes=[
            pltpu.VMEM((PER * BLOCK, COLS), F32),
            pltpu.SMEM((1, POSITIONS), I32),
            pltpu.SMEM((1, DEVS), I32),
            pltpu.VMEM((1, POSITIONS, BLOCK), I32),
            pltpu.VMEM((1, POSITIONS, BLOCK), I32),
            pltpu.VMEM((rows, COLS), F32),
            pltpu.VMEM((rows, COLS), BF16),
            pltpu.VMEM((rows, COLS), BF16),
            pltpu.VMEM((DEVS * SHARD, NB), F32),
            pltpu.SMEM((PER + 1,), I32),
            pltpu.SemaphoreType.DMA((4,)),
            pltpu.SemaphoreType.DMA((PER,)),
            pltpu.SemaphoreType.DMA((PER,)),
            pltpu.SemaphoreType.DMA((NBLK,)),
        ],
        compiler_params=pltpu.CompilerParams(vmem_limit_bytes=62 << 20),
        name="mix_rows",
    )(block_order, counts, matrix, sign_bits, row_mask)


def reduce_kernel(
    g, full, mine, acc, fwd, got, fwd_p, fwd_m, got2, own, z_buf, z_sum, z_all, mean,
    own_sem, pair_sem, rs_sem, z_sem, m_sem, swap_sem, ag_sem,
):
    grp = lax.axis_index("grp")
    dev = lax.axis_index("dev")
    core = lax.rem(dev, 2)
    chip = dev // 2
    cx, cy = chip // 4, lax.rem(chip, 4)
    partner = chip * 2 + 1 - core
    first = (cx, cy)
    second = (cy, cx)

    def mod4(i):
        return lax.rem(i + 4, 4)

    def neighbour(h, dim, step):
        if (h + dim) % 2 == 0:
            to = mod4(cx + step) * 4 + cy
        else:
            to = cx * 4 + mod4(cy + step)
        return to * 2 + core

    def copy(src, dst, sem, at, to_dev, to_grp=grp):
        return pltpu.make_async_remote_copy(
            src_ref=src,
            dst_ref=dst,
            send_sem=sem.at[(0, *at)],
            recv_sem=sem.at[(1, *at)],
            device_id=(to_grp, to_dev),
            device_id_type=MESH,
        )

    sent = []

    def send(*args):
        c = copy(*args)
        c.start()
        sent.append(c)

    def receive(dst, sem, at):
        copy(dst, dst, sem, at, partner).wait_recv()

    def z_start(z):
        return pl.multiple_of((z * 15) // 7 * 8, 8)

    def run(lo, hi, act):
        def step(d, c):
            act(d)
            return c

        lax.fori_loop(lo, hi, step, 0)

    keep = pltpu.make_async_copy(g.at[core], mine, own_sem)
    keep.start()
    barrier = pltpu.get_barrier_semaphore()

    def greet(to_dev, to_grp=grp):
        pl.semaphore_signal(barrier, inc=1, device_id=(to_grp, to_dev), device_id_type=MESH)

    greet(partner)
    for dim in range(2):
        for step in (1, -1):
            greet(neighbour(0, dim, step))
    run(1, GRPS, lambda d: greet(dev, lax.rem(grp + d, GRPS)))
    pl.semaphore_wait(barrier, 5 + GRPS - 1)

    steps = (2, 1, -1, 0)
    for i, step in enumerate(steps):
        for h in range(2):
            a = mod4(first[h] + step)
            send(g.at[1 - core, h, a], acc.at[h, a], pair_sem, (h, i), partner)
    keep.wait()

    def pair_sum(i):
        for h in range(2):
            a = mod4(first[h] + steps[i])
            receive(acc.at[h, a], pair_sem, (h, i))
            acc[h, a] = acc[h, a] + mine[h, a]

    lo, hi = pl.ds(0, 2), pl.ds(2, 2)
    pair_sum(0)
    for h in range(2):
        u = first[h]
        send(acc.at[h, mod4(u + 2), lo], fwd.at[h, 0], rs_sem, (h, 0), neighbour(h, 0, 1))
        send(acc.at[h, mod4(u + 2), hi], fwd.at[h, 1], rs_sem, (h, 1), neighbour(h, 0, -1))
    pair_sum(1)
    for h in range(2):
        send(acc.at[h, mod4(first[h] + 1), hi], got.at[h, 0, hi], rs_sem, (h, 2), neighbour(h, 0, 1))
    pair_sum(2)
    for h in range(2):
        send(acc.at[h, mod4(first[h] - 1), lo], got.at[h, 1, lo], rs_sem, (h, 3), neighbour(h, 0, -1))
    pair_sum(3)
    for h in range(2):
        up, down = mod4(first[h] + 1), mod4(first[h] - 1)
        receive(fwd.at[h, 0], rs_sem, (h, 0))
        acc[h, up, 0:2] = acc[h, up, 0:2] + fwd[h, 0]
        send(acc.at[h, up, lo], got.at[h, 0, lo], rs_sem, (h, 4), neighbour(h, 0, 1))
        receive(fwd.at[h, 1], rs_sem, (h, 1))
        acc[h, down, 2:4] = acc[h, down, 2:4] + fwd[h, 1]
        send(acc.at[h, down, hi], got.at[h, 1, hi], rs_sem, (h, 5), neighbour(h, 0, -1))
    top, bottom = pl.ds(0, CUT), pl.ds(CUT, HALF - CUT)
    for h in range(2):
        u, v = first[h], second[h]
        receive(got.at[h, 0, hi], rs_sem, (h, 2))
        receive(got.at[h, 1, lo], rs_sem, (h, 3))
        receive(got.at[h, 0, lo], rs_sem, (h, 4))
        receive(got.at[h, 1, hi], rs_sem, (h, 5))
        acc[h, u] = acc[h, u] + got[h, 0] + got[h, 1]
        send(acc.at[h, u, mod4(v + 2), top], fwd_p.at[h], rs_sem, (h, 6), neighbour(h, 1, 1))
        send(acc.at[h, u, mod4(v + 2), bottom], fwd_m.at[h], rs_sem, (h, 7), neighbour(h, 1, -1))
        send(acc.at[h, u, mod4(v + 1), bottom], got2.at[h, 0, bottom], rs_sem, (h, 8), neighbour(h, 1, 1))
        send(acc.at[h, u, mod4(v - 1), top], got2.at[h, 1, top], rs_sem, (h, 9), neighbour(h, 1, -1))
    for h in range(2):
        u, up, down = first[h], mod4(second[h] + 1), mod4(second[h] - 1)
        receive(fwd_p.at[h], rs_sem, (h, 6))
        acc[h, u, up, 0:CUT] = acc[h, u, up, 0:CUT] + fwd_p[h]
        send(acc.at[h, u, up, top], got2.at[h, 0, top], rs_sem, (h, 10), neighbour(h, 1, 1))
        receive(fwd_m.at[h], rs_sem, (h, 7))
        acc[h, u, down, CUT:HALF] = acc[h, u, down, CUT:HALF] + fwd_m[h]
        send(acc.at[h, u, down, bottom], got2.at[h, 1, bottom], rs_sem, (h, 11), neighbour(h, 1, -1))
    for h in range(2):
        receive(got2.at[h, 0, bottom], rs_sem, (h, 8))
        receive(got2.at[h, 1, top], rs_sem, (h, 9))
        receive(got2.at[h, 0, top], rs_sem, (h, 10))
        receive(got2.at[h, 1, bottom], rs_sem, (h, 11))
        total = acc[h, first[h], second[h]] + got2[h, 0] + got2[h, 1]
        own[h * HALF : (h + 1) * HALF, :] = total * (1.0 / (POSITIONS * KEEP))

    def z_copy(d):
        to = lax.rem(grp + d, GRPS)
        return copy(own.at[pl.ds(z_start(to), ZROWS)], z_buf.at[d], z_sem, (d,), dev, to)

    run(1, GRPS, lambda d: z_copy(d).start())

    def block(h):
        return full.at[h, first[h], second[h], core]

    def swap(src, h):
        return copy(src.at[pl.ds(h * HALF, HALF)], block(h), swap_sem, (h,), partner)

    @pl.when(core == 1)
    def _():
        for h in range(2):
            swap(own, h).start()

    run(1, GRPS, lambda d: z_copy(d).wait())
    total = own[pl.ds(z_start(grp), ZROWS), :]
    for d in range(1, GRPS):
        total = total + z_buf[d]
    z_sum[...] = total * (1.0 / GRPS)

    def m_copy(d):
        return copy(z_sum, z_all.at[grp], m_sem, (d,), dev, lax.rem(grp + d, GRPS))

    run(1, GRPS, lambda d: m_copy(d).start())
    z_all[grp] = z_sum[...]

    def m_receive(d):
        receive(z_all.at[lax.rem(grp + GRPS - d, GRPS)], m_sem, (d,))

    run(1, GRPS, m_receive)
    for z in range(GRPS):
        at = (z * 15) // 7 * 8
        mean[at : at + ZROWS, :] = z_all[z]

    @pl.when(core == 0)
    def _():
        for h in range(2):
            swap(mean, h).start()
            full[h, first[h], second[h], 0] = own[h * HALF : (h + 1) * HALF, :]

    @pl.when(core == 1)
    def _():
        for h in range(2):
            full[h, first[h], second[h], 1] = mean[h * HALF : (h + 1) * HALF, :]

    for h in range(2):
        receive(full.at[h, first[h], second[h], 1 - core], swap_sem, (h,))

    def spread(piece, slot, h, dim):
        send(piece, piece, ag_sem, (h, slot), neighbour(h, dim, 1))
        send(piece, piece, ag_sem, (h, slot + 1), neighbour(h, dim, -1))

    def forward(before, after, slot, h, dim):
        receive(before, ag_sem, (h, slot))
        receive(after, ag_sem, (h, slot + 1))
        send(before.at[0], before.at[0], ag_sem, (h, slot + 2), neighbour(h, dim, 1))
        send(after.at[1], after.at[1], ag_sem, (h, slot + 3), neighbour(h, dim, -1))

    def last(opposite, slot, h):
        receive(opposite.at[0], ag_sem, (h, slot + 2))
        receive(opposite.at[1], ag_sem, (h, slot + 3))

    def at(h, i, j):
        return full.at[h, mod4(first[h] + i), mod4(second[h] + j)]

    for h in range(2):
        spread(at(h, 0, 0), 0, h, 1)
    for h in range(2):
        spread(at(h, 0, 0), 4, h, 0)
    for h in range(2):
        forward(at(h, 0, -1), at(h, 0, 1), 0, h, 1)
    for h in range(2):
        spread(at(h, 0, -1), 8, h, 0)
        spread(at(h, 0, 1), 12, h, 0)
    for h in range(2):
        forward(at(h, -1, 0), at(h, 1, 0), 4, h, 0)
        last(at(h, 0, 2), 0, h)
        spread(at(h, 0, 2), 16, h, 0)
    for j, slot in ((-1, 8), (1, 12), (2, 16)):
        for h in range(2):
            forward(at(h, -1, j), at(h, 1, j), slot, h, 0)
    for j, slot in ((0, 4), (-1, 8), (1, 12), (2, 16)):
        for h in range(2):
            last(at(h, 2, j), slot, h)

    run(1, GRPS, lambda d: m_copy(d).wait_send())
    for h in range(2):
        swap(own, h).wait_send()
    for c in sent:
        c.wait_send()


def reduce_gram(gram):
    dma = pltpu.SemaphoreType.DMA
    vmem = lambda *shape: pltpu.VMEM((*shape, NB), F32)
    return pl.pallas_call(
        reduce_kernel,
        out_shape=jax.ShapeDtypeStruct((2, 4, 4, 2, HALF, NB), F32),
        in_specs=[pl.BlockSpec(memory_space=pltpu.HBM)],
        out_specs=pl.BlockSpec(memory_space=pltpu.VMEM),
        scratch_shapes=[
            vmem(2, 4, 4, HALF),
            vmem(2, 4, 4, HALF),
            vmem(2, 2, 2, HALF),
            vmem(2, 2, 4, HALF),
            vmem(2, CUT),
            vmem(2, HALF - CUT),
            vmem(2, 2, HALF),
            vmem(SHARD),
            vmem(GRPS, ZROWS),
            vmem(ZROWS),
            vmem(GRPS, ZROWS),
            vmem(SHARD),
            dma,
            dma((2, 2, 4)),
            dma((2, 2, 12)),
            dma((2, GRPS)),
            dma((2, GRPS)),
            dma((2, 2)),
            dma((2, 2, 20)),
        ],
        compiler_params=pltpu.CompilerParams(
            collective_id=0, has_side_effects=True, vmem_limit_bytes=61 << 20
        ),
        name="reduce_gram",
    )(gram.reshape(2, 2, 4, 4, HALF, NB))


def diag_factor(d):
    n = NB // 8
    lane = lax.broadcasted_iota(I32, (8, NB), 1)
    sub = lax.broadcasted_iota(I32, (8, NB), 0)

    def column(x, i):
        return jnp.broadcast_to(x[:, i : i + 1], (8, NB))

    def line(x, i):
        return jnp.broadcast_to(x[i : i + 1, :], (8, NB))

    t_rows = [d[8 * s : 8 * s + 8, :] for s in range(n)]
    e_rows = [jnp.where(lane == sub + 8 * s, 1.0, 0.0).astype(F32) for s in range(n)]
    r_out, e_out = [], []
    low, scale, r_lines, e_lines = {}, [], [], []
    for s in range(n):
        c0 = 8 * s
        t, e = t_rows[s], e_rows[s]
        cols = [column(t, c0 + j) for j in range(8)]
        if s:
            before = []
            for j in range(8):
                c = column(t_rows[s], c0 - 8 + j)
                for m in range(j):
                    c = c - before[m] * low[m, j]
                before.append(c * scale[j])
            for j in range(8):
                c = before[j]
                t = t - c * r_lines[j]
                e = e - c * e_lines[j]
                cols = [x - c * line(c, k) for k, x in enumerate(cols)]
        b = {(i, j): line(cols[j], i) for i in range(8) for j in range(i, 8)}
        rows = [line(t, j) for j in range(8)]
        extra = [line(e, j) for j in range(8)]
        low, scale, r_lines, e_lines = {}, [], [], []
        r_strip = e_strip = None
        for j in range(8):
            q = lax.rsqrt(b[j, j])
            scale.append(q)
            for k in range(j + 1, 8):
                low[j, k] = b[j, k] * q
            for i in range(j + 1, 8):
                for k in range(i, 8):
                    b[i, k] = b[i, k] - low[j, i] * low[j, k]
            rj, ej = rows[j] * q, extra[j] * q
            r_lines.append(rj)
            e_lines.append(ej)
            for i in range(j + 1, 8):
                rows[i] = rows[i] - low[j, i] * rj
                extra[i] = extra[i] - low[j, i] * ej
            r_strip = rj if j == 0 else jnp.where(sub == j, rj, r_strip)
            e_strip = ej if j == 0 else jnp.where(sub == j, ej, e_strip)
        r_out.append(r_strip)
        e_out.append(e_strip)
        if s + 2 >= n:
            continue
        w = jnp.concatenate([r_strip, e_strip], axis=1)
        h = w.astype(BF16).astype(F32)
        rest = w - h
        m = rest.astype(BF16).astype(F32)
        q = rest - m
        lhs = jnp.concatenate([v[:, :NB] for v in (h, h, m, m, h, q)], axis=0).astype(BF16)
        rhs = jnp.concatenate([h, m, h, m, q, h], axis=0).astype(BF16)
        update = dot_t(lhs, rhs)
        for i in range(s + 2, n):
            t_rows[i] = t_rows[i] - update[8 * i : 8 * i + 8, :NB]
            e_rows[i] = e_rows[i] - update[8 * i : 8 * i + 8, NB:]
    return jnp.concatenate(r_out, axis=0), jnp.concatenate(e_out, axis=0)


def cholesky_kernel(g, out, a, r, d):
    for i in range(NBLK):
        for j in range(i, NBLK):
            at = packed(i, j) * NB
            row, end = 0, NB
            while row < end:
                shard, start = divmod(at + row, HALF)
                size = min(HALF - start, end - row)
                half, chip = shard // CHIPS % 2, shard % CHIPS
                part = g[half, chip // 4, chip % 4, shard // (2 * CHIPS), start : start + size, :]
                a[i * NB + row : i * NB + row + size, j * NB : (j + 1) * NB] = part
                row += size
    row = lax.broadcasted_iota(I32, (NB, NB), 0)
    col = lax.broadcasted_iota(I32, (NB, NB), 1)
    d[...] = a[0:NB, 0:NB]

    def step(k, c):
        top, inverse = diag_factor(d[...])
        d[...] = jnp.where(row <= col, top, 0.0)
        hi, mid = split2(inverse)
        left = jnp.concatenate([hi, hi, mid], axis=1)
        for kk in range(NBLK):

            @pl.when(k == kk)
            def _():
                k0, k1 = kk * NB, (kk + 1) * NB
                r[k0:k1, k0:k1] = d[...]
                if kk:
                    r[k0:k1, 0:k0] = jnp.zeros((NB, k0), F32)
                if kk == NBLK - 1:
                    return
                hi, mid = split2(a[k0:k1, k1:])
                strip = dot_n(left, jnp.concatenate([hi, mid, hi], axis=0))
                r[k0:k1, k1:] = strip
                hi, mid = split2(strip)
                lhs = jnp.concatenate([hi, hi, mid], axis=0)
                rhs = jnp.concatenate([hi, mid, hi], axis=0)
                d[...] = a[k1 : k1 + NB, k1 : k1 + NB] - dot_t(lhs[:, :NB], rhs[:, :NB])
                for i in range((COLS - k1) // NB):
                    lo, hi_ = i * NB, (i + 1) * NB
                    if i:
                        a[k1 + lo : k1 + hi_, k1 + lo :] -= dot_t(lhs[:, lo:hi_], rhs[:, lo:])
                    elif kk < NBLK - 2:
                        a[k1 : k1 + NB, k1 + NB :] -= dot_t(lhs[:, :NB], rhs[:, NB:])

        return c

    lax.fori_loop(0, NBLK, step, 0)
    chip = lax.axis_index("dev") // 2
    out[...] = r[pl.ds(pl.multiple_of(chip * 64, 64), 64), :]


def cholesky_rows(full):
    vmem = pl.BlockSpec(memory_space=pltpu.VMEM)
    return pl.pallas_call(
        cholesky_kernel,
        out_shape=jax.ShapeDtypeStruct((2 * COLS // DEVS, COLS), F32),
        in_specs=[vmem],
        out_specs=vmem,
        scratch_shapes=[
            pltpu.VMEM((COLS, COLS), F32),
            pltpu.VMEM((COLS, COLS), F32),
            pltpu.VMEM((NB, NB), F32),
        ],
        compiler_params=pltpu.CompilerParams(vmem_limit_bytes=32 << 20),
        cost_estimate=pl.CostEstimate(flops=50_000_000_000, bytes_accessed=100_000_000, transcendentals=0),
        name="cholesky_rows",
    )(full)


def place_kernel(order_in, counts_in, arrived, sketch, order, counts, stage, zero, tab_sem, in_sem, sem):
    me = lax.axis_index("dev")
    tables = [
        pltpu.make_async_copy(order_in, order, tab_sem.at[0]),
        pltpu.make_async_copy(counts_in, counts, tab_sem.at[1]),
    ]
    for table in tables:
        table.start()
    zero[...] = jnp.zeros_like(zero)
    for table in tables:
        table.wait()

    def add(e, c):
        return c + jnp.where(e < me, counts[0, e], 0)

    offset = lax.fori_loop(0, DEVS, add, jnp.int32(0))
    held = counts[0, me]

    def load(j):
        source = order[0, jnp.minimum(offset + j, POSITIONS - 1)] >> 4
        return pltpu.make_async_copy(arrived.at[source], stage.at[j], in_sem.at[j])

    def start(j, c):
        @pl.when(j < held)
        def _():
            load(j).start()

        @pl.when(j >= held)
        def _():
            pltpu.make_async_copy(zero, sketch.at[j], sem.at[j]).start()

        return c

    def store(j, c):
        @pl.when(j < held)
        def _():
            load(j).wait()
            pltpu.make_async_copy(stage.at[j], sketch.at[j], sem.at[j]).start()

        return c

    def wait(j, c):
        pltpu.make_async_copy(zero, sketch.at[j], sem.at[j]).wait()
        return c

    lax.fori_loop(0, DEVS, start, 0)
    lax.fori_loop(0, DEVS, store, 0)
    lax.fori_loop(0, DEVS, wait, 0)


def place(block_order, counts, arrived):
    hbm = pl.BlockSpec(memory_space=pltpu.HBM)
    return pl.pallas_call(
        place_kernel,
        out_shape=jax.ShapeDtypeStruct((DEVS, KEEP, COLS), F32),
        in_specs=[hbm] * 3,
        out_specs=hbm,
        scratch_shapes=[
            pltpu.SMEM((1, POSITIONS), I32),
            pltpu.SMEM((1, DEVS), I32),
            pltpu.VMEM((DEVS, KEEP, COLS), F32),
            pltpu.VMEM((KEEP, COLS), F32),
            pltpu.SemaphoreType.DMA((2,)),
            pltpu.SemaphoreType.DMA((DEVS,)),
            pltpu.SemaphoreType.DMA((DEVS,)),
        ],
        compiler_params=pltpu.CompilerParams(vmem_limit_bytes=16 << 20),
        name="place_slots",
    )(block_order, counts, arrived)


def body(matrix, block_order, counts, sign_bits, row_mask):
    send, gram = mix(matrix, block_order, counts, sign_bits, row_mask)
    full = reduce_gram(gram)
    send, full = lax.optimization_barrier((send, full))
    arrived = lax.all_to_all(send, "dev", split_axis=0, concat_axis=0, tiled=True)
    rows = cholesky_rows(full)
    half = rows.shape[0] // 2
    first = lax.rem(lax.axis_index("dev"), 2) == 0
    mine = jnp.where(first, rows[:half], rows[half:])
    other = jnp.where(first, rows[half:], rows[:half])
    other = lax.ppermute(other, "dev", [(d, d ^ 1) for d in range(DEVS)])
    sketch = place(block_order, counts, arrived)
    group_factor = jnp.where(first, mine, other)[None]
    factor = jnp.where(first, other, mine)
    return sketch.reshape(DEVS * KEEP, COLS), group_factor, factor


def solution(mesh):
    placed = (
        P(("grp", "dev"), None),
        P("grp", None),
        P("grp", None),
        P("grp", None, None),
        P("grp", None, None),
    )
    return jax.shard_map(
        body,
        mesh=mesh,
        in_specs=placed,
        out_specs=(P(("grp", "dev"), None), P("grp", "dev", None), P("dev", None)),
        check_vma=False,
    )
```

```python
import jax
import jax.numpy as jnp
from jax import lax
from jax.experimental import pallas as pl
from jax.experimental.pallas import tpu as pltpu
from jax.sharding import PartitionSpec as P

MESH = pl.DeviceIdType.MESH
F32, BF16, I32 = jnp.float32, jnp.bfloat16, jnp.int32
BLOCK = 128
KEEP = 32
NB = 128
COLS = 1024
NBLK = COLS // NB
PER = 16
POSITIONS = 512
DEVS = 32
GRPS = 8
CHIPS = 16
SHARD = NBLK * (NBLK + 1) // 2 * NB // DEVS
ZROWS = 24
HALF = SHARD // 2
CUT = 40
EARLY = 8

OTHERS = [
    (x, y, c)
    for c in range(2)
    for x, y in ((1, 0), (0, 1), (3, 0), (0, 3), (1, 1), (3, 3), (1, 3), (3, 1), (2, 0), (0, 2), (2, 1), (1, 2), (2, 3), (3, 2), (2, 2))
] + [(0, 0, 1)]
GAPS = (14, 0, 0, 9, 8)


def packed(i, j):
    return i * NBLK - i * (i - 1) // 2 + (j - i)


def split2(x):
    h = x.astype(BF16)
    return h, (x - h.astype(F32)).astype(BF16)


def dot_t(a, b):
    return lax.dot_general(a, b, (((0,), (0,)), ((), ())), preferred_element_type=F32)


def dot_n(a, b):
    return lax.dot_general(a, b, (((1,), (0,)), ((), ())), preferred_element_type=F32)


def mix_kernel(order_in, counts_in, matrix, sign_bits, row_mask, send_a, send_b, gram, x, order, counts, signs, masks, s_rows, s_hi, s_mid, gram_v, place, tab_sem, in_sem, out_sem, gram_sem):
    me = lax.axis_index("dev")

    def fetch(k):
        return pltpu.make_async_copy(
            matrix.at[pl.ds(k * BLOCK, BLOCK)], x.at[pl.ds(k * BLOCK, BLOCK)], in_sem.at[k]
        )

    pairs = ((order_in, order), (counts_in, counts), (sign_bits, signs), (row_mask, masks))
    tables = [pltpu.make_async_copy(a, b, tab_sem.at[i]) for i, (a, b) in enumerate(pairs)]
    for table in tables:
        table.start()
    for k in range(PER):
        fetch(k).start()
    tables[0].wait()
    tables[1].wait()

    def find(p, carry):
        b = order[0, p]
        place[jnp.where((b >> 4) == me, b & 15, PER)] = p
        return carry

    lax.fori_loop(0, POSITIONS, find, 0, unroll=8)
    pos = [place[k] for k in range(PER)]

    def count(e, carry):
        run, owners = carry
        run = run + counts[0, e]
        return run, tuple(o + (p >= run).astype(I32) for o, p in zip(owners, pos))

    _, owners = lax.fori_loop(0, DEVS, count, (jnp.int32(0), (jnp.int32(0),) * PER))

    row = lax.broadcasted_iota(I32, (BLOCK, BLOCK), 0)
    col = lax.broadcasted_iota(I32, (BLOCK, BLOCK), 1)
    parity = row & col
    for shift in (4, 2, 1):
        parity = parity ^ (parity >> shift)
    walsh = (1 - 2 * (parity & 1)).astype(F32).astype(BF16)
    upto = jnp.where(row <= col, 1.0, 0.0).astype(BF16)
    tables[2].wait()
    tables[3].wait()
    mask = jnp.concatenate([masks[0, pl.ds(p, 1), :] for p in pos], axis=0).astype(F32)
    sign = jnp.concatenate([signs[0, pl.ds(p, 1), :] for p in pos], axis=0)
    sign = (1 - 2 * sign).astype(F32)
    running = dot_n(mask.astype(BF16), upto).astype(I32)
    nth = lax.broadcasted_iota(I32, (KEEP, BLOCK), 0) + 1
    chosen = [
        jnp.where((running[k : k + 1] == nth) & (mask[k : k + 1] > 0.5), 1.0, 0.0) for k in range(PER)
    ]
    mixing = dot_n(jnp.concatenate(chosen, axis=0).astype(BF16), walsh)

    outs = []
    for k in range(PER):
        t = (mixing[k * KEEP : (k + 1) * KEEP] * sign[k : k + 1]).astype(BF16)
        fetch(k).wait()
        block = x[k * BLOCK : (k + 1) * BLOCK, :]
        hi = block.astype(BF16)
        rest = block - hi.astype(F32)
        mid = rest.astype(BF16)
        low = (rest - mid.astype(F32)).astype(BF16)
        mixed = dot_n(t, hi) + dot_n(t, mid) + dot_n(t, low)
        mixed = mixed * float(BLOCK) ** -0.5
        rows = slice(k * KEEP, (k + 1) * KEEP)
        s_rows[rows, :] = mixed
        hi, mid = split2(mixed)
        s_hi[rows, :] = hi
        s_mid[rows, :] = mid
        cut = k * KEEP + EARLY
        for i, part, send in ((0, pl.ds(k * KEEP, EARLY), send_a), (1, pl.ds(cut, KEEP - EARLY), send_b)):
            out = pltpu.make_async_copy(s_rows.at[part], send.at[owners[k]], out_sem.at[k, i])
            out.start()
            outs.append(out)

    for i in range(NBLK):
        a, b = i * NB, (i + 1) * NB
        block = dot_t(s_hi[:, a:b], s_hi[:, a:]) + dot_t(s_hi[:, a:b], s_mid[:, a:])
        block = block + dot_t(s_mid[:, a:b], s_hi[:, a:])
        for j in range(i, NBLK):
            at = packed(i, j) * NB
            gram_v[at : at + NB, :] = block[:, (j - i) * NB : (j - i + 1) * NB]
        rows = pl.ds(packed(i, i) * NB, (NBLK - i) * NB)
        out = pltpu.make_async_copy(gram_v.at[rows], gram.at[rows], gram_sem.at[i])
        out.start()
        outs.append(out)
    for out in outs:
        out.wait()


def mix(matrix, block_order, counts, sign_bits, row_mask):
    hbm = pl.BlockSpec(memory_space=pltpu.HBM)
    rows = PER * KEEP
    return pl.pallas_call(
        mix_kernel,
        out_shape=(
            jax.ShapeDtypeStruct((DEVS, EARLY, COLS), F32),
            jax.ShapeDtypeStruct((DEVS, KEEP - EARLY, COLS), F32),
            jax.ShapeDtypeStruct((DEVS * SHARD, NB), F32),
        ),
        in_specs=[hbm] * 5,
        out_specs=(hbm, hbm, hbm),
        scratch_shapes=[
            pltpu.VMEM((PER * BLOCK, COLS), F32),
            pltpu.SMEM((1, POSITIONS), I32),
            pltpu.SMEM((1, DEVS), I32),
            pltpu.VMEM((1, POSITIONS, BLOCK), I32),
            pltpu.VMEM((1, POSITIONS, BLOCK), I32),
            pltpu.VMEM((rows, COLS), F32),
            pltpu.VMEM((rows, COLS), BF16),
            pltpu.VMEM((rows, COLS), BF16),
            pltpu.VMEM((DEVS * SHARD, NB), F32),
            pltpu.SMEM((PER + 1,), I32),
            pltpu.SemaphoreType.DMA((4,)),
            pltpu.SemaphoreType.DMA((PER,)),
            pltpu.SemaphoreType.DMA((PER, 2)),
            pltpu.SemaphoreType.DMA((NBLK,)),
        ],
        compiler_params=pltpu.CompilerParams(vmem_limit_bytes=62 << 20),
        name="mix_rows",
    )(block_order, counts, matrix, sign_bits, row_mask)


def reduce_kernel(
    g, blocks, full, arrived, mine, acc, fwd, got, fwd_p, fwd_m, got2, own, z_buf, z_sum, z_all, mean,
    own_sem, pair_sem, rs_sem, z_sem, m_sem, swap_sem, ag_sem, all_sem, stay_sem,
):
    grp = lax.axis_index("grp")
    dev = lax.axis_index("dev")
    core = lax.rem(dev, 2)
    chip = dev // 2
    cx, cy = chip // 4, lax.rem(chip, 4)
    partner = chip * 2 + 1 - core
    first = (cx, cy)
    second = (cy, cx)

    def mod4(i):
        return lax.rem(i + 4, 4)

    def at_offset(dx, dy, flip=0):
        return (mod4(cx + dx) * 4 + mod4(cy + dy)) * 2 + lax.rem(core + flip, 2)

    def neighbour(h, dim, step):
        return at_offset(step, 0) if (h + dim) % 2 == 0 else at_offset(0, step)

    def copy(src, dst, sem, at, to_dev, to_grp=grp):
        return pltpu.make_async_remote_copy(
            src_ref=src,
            dst_ref=dst,
            send_sem=sem.at[(0, *at)],
            recv_sem=sem.at[(1, *at)],
            device_id=(to_grp, to_dev),
            device_id_type=MESH,
        )

    sent = []

    def send(*args):
        c = copy(*args)
        c.start()
        sent.append(c)

    def receive(dst, sem, at):
        copy(dst, dst, sem, at, partner).wait_recv()

    def z_start(z):
        return pl.multiple_of((z * 15) // 7 * 8, 8)

    def run(lo, hi, act):
        def step(d, c):
            act(d)
            return c

        lax.fori_loop(lo, hi, step, 0)

    keep = pltpu.make_async_copy(g.at[core], mine, own_sem)
    keep.start()
    barrier = pltpu.get_barrier_semaphore()

    def greet(to_dev, to_grp=grp):
        pl.semaphore_signal(barrier, inc=1, device_id=(to_grp, to_dev), device_id_type=MESH)

    for others in OTHERS:
        greet(at_offset(*others))
    run(1, GRPS, lambda d: greet(dev, lax.rem(grp + d, GRPS)))
    pl.semaphore_wait(barrier, len(OTHERS) + GRPS - 1)

    def block_copy(i):
        to = at_offset(*OTHERS[i])
        return copy(blocks.at[to], arrived.at[dev], all_sem, (i,), to)

    pending = list(range(len(OTHERS)))

    def fill(count):
        for _ in range(min(count, len(pending))):
            block_copy(pending.pop(0)).start()

    steps = (2, 1, -1, 0)
    for i, step in enumerate(steps):
        for h in range(2):
            a = mod4(first[h] + step)
            send(g.at[1 - core, h, a], acc.at[h, a], pair_sem, (h, i), partner)
    stay = pltpu.make_async_copy(blocks.at[dev], arrived.at[dev], stay_sem)
    stay.start()
    fill(GAPS[0])
    keep.wait()

    def pair_sum(i):
        for h in range(2):
            a = mod4(first[h] + steps[i])
            receive(acc.at[h, a], pair_sem, (h, i))
            acc[h, a] = acc[h, a] + mine[h, a]

    lo, hi = pl.ds(0, 2), pl.ds(2, 2)
    pair_sum(0)
    for h in range(2):
        u = first[h]
        send(acc.at[h, mod4(u + 2), lo], fwd.at[h, 0], rs_sem, (h, 0), neighbour(h, 0, 1))
        send(acc.at[h, mod4(u + 2), hi], fwd.at[h, 1], rs_sem, (h, 1), neighbour(h, 0, -1))
    pair_sum(1)
    for h in range(2):
        send(acc.at[h, mod4(first[h] + 1), hi], got.at[h, 0, hi], rs_sem, (h, 2), neighbour(h, 0, 1))
    pair_sum(2)
    for h in range(2):
        send(acc.at[h, mod4(first[h] - 1), lo], got.at[h, 1, lo], rs_sem, (h, 3), neighbour(h, 0, -1))
    pair_sum(3)
    for h in range(2):
        up, down = mod4(first[h] + 1), mod4(first[h] - 1)
        receive(fwd.at[h, 0], rs_sem, (h, 0))
        acc[h, up, 0:2] = acc[h, up, 0:2] + fwd[h, 0]
        send(acc.at[h, up, lo], got.at[h, 0, lo], rs_sem, (h, 4), neighbour(h, 0, 1))
        receive(fwd.at[h, 1], rs_sem, (h, 1))
        acc[h, down, 2:4] = acc[h, down, 2:4] + fwd[h, 1]
        send(acc.at[h, down, hi], got.at[h, 1, hi], rs_sem, (h, 5), neighbour(h, 0, -1))
    fill(GAPS[1])
    top, bottom = pl.ds(0, CUT), pl.ds(CUT, HALF - CUT)
    for h in range(2):
        u, v = first[h], second[h]
        receive(got.at[h, 0, hi], rs_sem, (h, 2))
        receive(got.at[h, 1, lo], rs_sem, (h, 3))
        receive(got.at[h, 0, lo], rs_sem, (h, 4))
        receive(got.at[h, 1, hi], rs_sem, (h, 5))
        acc[h, u] = acc[h, u] + got[h, 0] + got[h, 1]
        send(acc.at[h, u, mod4(v + 2), top], fwd_p.at[h], rs_sem, (h, 6), neighbour(h, 1, 1))
        send(acc.at[h, u, mod4(v + 2), bottom], fwd_m.at[h], rs_sem, (h, 7), neighbour(h, 1, -1))
        send(acc.at[h, u, mod4(v + 1), bottom], got2.at[h, 0, bottom], rs_sem, (h, 8), neighbour(h, 1, 1))
        send(acc.at[h, u, mod4(v - 1), top], got2.at[h, 1, top], rs_sem, (h, 9), neighbour(h, 1, -1))
    for h in range(2):
        u, up, down = first[h], mod4(second[h] + 1), mod4(second[h] - 1)
        receive(fwd_p.at[h], rs_sem, (h, 6))
        acc[h, u, up, 0:CUT] = acc[h, u, up, 0:CUT] + fwd_p[h]
        send(acc.at[h, u, up, top], got2.at[h, 0, top], rs_sem, (h, 10), neighbour(h, 1, 1))
        receive(fwd_m.at[h], rs_sem, (h, 7))
        acc[h, u, down, CUT:HALF] = acc[h, u, down, CUT:HALF] + fwd_m[h]
        send(acc.at[h, u, down, bottom], got2.at[h, 1, bottom], rs_sem, (h, 11), neighbour(h, 1, -1))
    fill(GAPS[2])
    for h in range(2):
        receive(got2.at[h, 0, bottom], rs_sem, (h, 8))
        receive(got2.at[h, 1, top], rs_sem, (h, 9))
        receive(got2.at[h, 0, top], rs_sem, (h, 10))
        receive(got2.at[h, 1, bottom], rs_sem, (h, 11))
        total = acc[h, first[h], second[h]] + got2[h, 0] + got2[h, 1]
        own[h * HALF : (h + 1) * HALF, :] = total * (1.0 / (POSITIONS * KEEP))

    def z_copy(d):
        to = lax.rem(grp + d, GRPS)
        return copy(own.at[pl.ds(z_start(to), ZROWS)], z_buf.at[d], z_sem, (d,), dev, to)

    run(1, GRPS, lambda d: z_copy(d).start())

    def block(h):
        return full.at[h, first[h], second[h], core]

    def swap(src, h):
        return copy(src.at[pl.ds(h * HALF, HALF)], block(h), swap_sem, (h,), partner)

    def spreads(i, h):
        def at(i, j):
            return full.at[h, mod4(first[h] + i), mod4(second[h] + j)]

        def both(piece, slot, dim):
            return [(piece, slot, dim, 1), (piece, slot + 1, dim, -1)]

        def on(before, after, slot, dim):
            return [(before.at[0], slot + 2, dim, 1), (after.at[1], slot + 3, dim, -1)]

        if i == 0:
            return both(at(0, 0), 0, 1) + both(at(0, 0), 4, 0)
        if i == 1:
            return on(at(0, -1), at(0, 1), 0, 1) + both(at(0, -1), 8, 0) + both(at(0, 1), 12, 0)
        if i == 2:
            return on(at(-1, 0), at(1, 0), 4, 0) + both(at(0, 2), 16, 0)
        return [x for j, slot in ((-1, 8), (1, 12), (2, 16)) for x in on(at(-1, j), at(1, j), slot, 0)]

    def needs(i, h):
        def at(i, j):
            return full.at[h, mod4(first[h] + i), mod4(second[h] + j)]

        if i == 0:
            return []
        if i == 1:
            return [(at(0, -1), 0), (at(0, 1), 1)]
        if i == 2:
            return [(at(-1, 0), 4), (at(1, 0), 5), (at(0, 2).at[0], 2), (at(0, 2).at[1], 3)]
        if i == 3:
            return [x for j, slot in ((-1, 8), (1, 12), (2, 16)) for x in ((at(-1, j), slot), (at(1, j), slot + 1))]
        return [
            x
            for j, slot in ((0, 4), (-1, 8), (1, 12), (2, 16))
            for x in ((at(2, j).at[0], slot + 2), (at(2, j).at[1], slot + 3))
        ]

    def leave(piece, slot, h, dim, step):
        return copy(piece, piece, ag_sem, (h, slot), neighbour(h, dim, step))

    def stage(i):
        for h in range(2):
            for piece, slot in needs(i, h):
                receive(piece, ag_sem, (h, slot))
            if i < 4:
                for piece, slot, dim, step in spreads(i, h):
                    leave(piece, slot, h, dim, step).start()

    def begin(src):
        for h in range(2):
            full[h, first[h], second[h], core] = src[h * HALF : (h + 1) * HALF, :]
        for h in range(2):
            receive(full.at[h, first[h], second[h], 1 - core], swap_sem, (h,))
        stage(0)

    @pl.when(core == 1)
    def _():
        for h in range(2):
            swap(own, h).start()

    fill(GAPS[3])

    @pl.when(core == 0)
    def _():
        begin(own)

    run(1, GRPS, lambda d: z_copy(d).wait())
    total = own[pl.ds(z_start(grp), ZROWS), :]
    for d in range(1, GRPS):
        total = total + z_buf[d]
    z_sum[...] = total * (1.0 / GRPS)

    def m_copy(d):
        return copy(z_sum, z_all.at[grp], m_sem, (d,), dev, lax.rem(grp + d, GRPS))

    run(1, GRPS, lambda d: m_copy(d).start())
    z_all[grp] = z_sum[...]
    fill(GAPS[4])

    @pl.when(core == 0)
    def _():
        stage(1)

    def m_receive(d):
        receive(z_all.at[lax.rem(grp + GRPS - d, GRPS)], m_sem, (d,))

    run(1, GRPS, m_receive)
    for z in range(GRPS):
        start = (z * 15) // 7 * 8
        mean[start : start + ZROWS, :] = z_all[z]

    @pl.when(core == 0)
    def _():
        for h in range(2):
            swap(mean, h).start()

    @pl.when(core == 1)
    def _():
        begin(mean)
        stage(1)

    fill(len(OTHERS))
    stage(2)
    stage(3)
    stage(4)

    run(1, GRPS, lambda d: m_copy(d).wait_send())
    for h in range(2):
        swap(own, h).wait_send()
        for i in range(4):
            for piece, slot, dim, step in spreads(i, h):
                leave(piece, slot, h, dim, step).wait_send()
    for c in sent:
        c.wait_send()
    for i in range(len(OTHERS)):
        dx, dy, flip = OTHERS[i]
        copy(blocks.at[dev], arrived.at[at_offset(-dx, -dy, flip)], all_sem, (i,), partner).wait_recv()
        block_copy(i).wait_send()
    stay.wait()


def reduce_gram(gram, blocks):
    dma = pltpu.SemaphoreType.DMA
    vmem = lambda *shape: pltpu.VMEM((*shape, NB), F32)
    return pl.pallas_call(
        reduce_kernel,
        out_shape=(
            jax.ShapeDtypeStruct((2, 4, 4, 2, HALF, NB), F32),
            jax.ShapeDtypeStruct(blocks.shape, F32),
        ),
        in_specs=[pl.BlockSpec(memory_space=pltpu.HBM)] * 2,
        out_specs=(pl.BlockSpec(memory_space=pltpu.VMEM), pl.BlockSpec(memory_space=pltpu.HBM)),
        scratch_shapes=[
            vmem(2, 4, 4, HALF),
            vmem(2, 4, 4, HALF),
            vmem(2, 2, 2, HALF),
            vmem(2, 2, 4, HALF),
            vmem(2, CUT),
            vmem(2, HALF - CUT),
            vmem(2, 2, HALF),
            vmem(SHARD),
            vmem(GRPS, ZROWS),
            vmem(ZROWS),
            vmem(GRPS, ZROWS),
            vmem(SHARD),
            dma,
            dma((2, 2, 4)),
            dma((2, 2, 12)),
            dma((2, GRPS)),
            dma((2, GRPS)),
            dma((2, 2)),
            dma((2, 2, 20)),
            dma((2, len(OTHERS))),
            dma,
        ],
        compiler_params=pltpu.CompilerParams(
            collective_id=0, has_side_effects=True, vmem_limit_bytes=61 << 20
        ),
        name="reduce_gram",
    )(gram.reshape(2, 2, 4, 4, HALF, NB), blocks)


def diag_factor(d):
    n = NB // 8
    lane = lax.broadcasted_iota(I32, (8, NB), 1)
    sub = lax.broadcasted_iota(I32, (8, NB), 0)

    def column(x, i):
        return jnp.broadcast_to(x[:, i : i + 1], (8, NB))

    def line(x, i):
        return jnp.broadcast_to(x[i : i + 1, :], (8, NB))

    t_rows = [d[8 * s : 8 * s + 8, :] for s in range(n)]
    e_rows = [jnp.where(lane == sub + 8 * s, 1.0, 0.0).astype(F32) for s in range(n)]
    r_out, e_out = [], []
    low, scale, r_lines, e_lines = {}, [], [], []
    for s in range(n):
        c0 = 8 * s
        t, e = t_rows[s], e_rows[s]
        cols = [column(t, c0 + j) for j in range(8)]
        if s:
            before = []
            for j in range(8):
                c = column(t_rows[s], c0 - 8 + j)
                for m in range(j):
                    c = c - before[m] * low[m, j]
                before.append(c * scale[j])
            for j in range(8):
                c = before[j]
                t = t - c * r_lines[j]
                e = e - c * e_lines[j]
                cols = [x - c * line(c, k) for k, x in enumerate(cols)]
        b = {(i, j): line(cols[j], i) for i in range(8) for j in range(i, 8)}
        rows = [line(t, j) for j in range(8)]
        extra = [line(e, j) for j in range(8)]
        low, scale, r_lines, e_lines = {}, [], [], []
        r_strip = e_strip = None
        for j in range(8):
            q = lax.rsqrt(b[j, j])
            scale.append(q)
            for k in range(j + 1, 8):
                low[j, k] = b[j, k] * q
            for i in range(j + 1, 8):
                for k in range(i, 8):
                    b[i, k] = b[i, k] - low[j, i] * low[j, k]
            rj, ej = rows[j] * q, extra[j] * q
            r_lines.append(rj)
            e_lines.append(ej)
            for i in range(j + 1, 8):
                rows[i] = rows[i] - low[j, i] * rj
                extra[i] = extra[i] - low[j, i] * ej
            r_strip = rj if j == 0 else jnp.where(sub == j, rj, r_strip)
            e_strip = ej if j == 0 else jnp.where(sub == j, ej, e_strip)
        r_out.append(r_strip)
        e_out.append(e_strip)
        if s + 2 >= n:
            continue
        w = jnp.concatenate([r_strip, e_strip], axis=1)
        h = w.astype(BF16).astype(F32)
        rest = w - h
        m = rest.astype(BF16).astype(F32)
        q = rest - m
        lhs = jnp.concatenate([v[:, :NB] for v in (h, h, m, m, h, q)], axis=0).astype(BF16)
        rhs = jnp.concatenate([h, m, h, m, q, h], axis=0).astype(BF16)
        update = dot_t(lhs, rhs)
        for i in range(s + 2, n):
            t_rows[i] = t_rows[i] - update[8 * i : 8 * i + 8, :NB]
            e_rows[i] = e_rows[i] - update[8 * i : 8 * i + 8, NB:]
    return jnp.concatenate(r_out, axis=0), jnp.concatenate(e_out, axis=0)


def cholesky_kernel(g, out, a, r, d):
    for i in range(NBLK):
        for j in range(i, NBLK):
            at = packed(i, j) * NB
            row, end = 0, NB
            while row < end:
                shard, start = divmod(at + row, HALF)
                size = min(HALF - start, end - row)
                half, chip = shard // CHIPS % 2, shard % CHIPS
                part = g[half, chip // 4, chip % 4, shard // (2 * CHIPS), start : start + size, :]
                a[i * NB + row : i * NB + row + size, j * NB : (j + 1) * NB] = part
                row += size
    row = lax.broadcasted_iota(I32, (NB, NB), 0)
    col = lax.broadcasted_iota(I32, (NB, NB), 1)
    d[...] = a[0:NB, 0:NB]

    def step(k, c):
        top, inverse = diag_factor(d[...])
        d[...] = jnp.where(row <= col, top, 0.0)
        hi, mid = split2(inverse)
        left = jnp.concatenate([hi, hi, mid], axis=1)
        for kk in range(NBLK):

            @pl.when(k == kk)
            def _():
                k0, k1 = kk * NB, (kk + 1) * NB
                r[k0:k1, k0:k1] = d[...]
                if kk:
                    r[k0:k1, 0:k0] = jnp.zeros((NB, k0), F32)
                if kk == NBLK - 1:
                    return
                hi, mid = split2(a[k0:k1, k1:])
                strip = dot_n(left, jnp.concatenate([hi, mid, hi], axis=0))
                r[k0:k1, k1:] = strip
                hi, mid = split2(strip)
                lhs = jnp.concatenate([hi, hi, mid], axis=0)
                rhs = jnp.concatenate([hi, mid, hi], axis=0)
                d[...] = a[k1 : k1 + NB, k1 : k1 + NB] - dot_t(lhs[:, :NB], rhs[:, :NB])
                for i in range((COLS - k1) // NB):
                    lo, hi_ = i * NB, (i + 1) * NB
                    if i:
                        a[k1 + lo : k1 + hi_, k1 + lo :] -= dot_t(lhs[:, lo:hi_], rhs[:, lo:])
                    elif kk < NBLK - 2:
                        a[k1 : k1 + NB, k1 + NB :] -= dot_t(lhs[:, :NB], rhs[:, NB:])

        return c

    lax.fori_loop(0, NBLK, step, 0)
    chip = lax.axis_index("dev") // 2
    out[...] = r[pl.ds(pl.multiple_of(chip * 64, 64), 64), :]


def cholesky_rows(full):
    vmem = pl.BlockSpec(memory_space=pltpu.VMEM)
    return pl.pallas_call(
        cholesky_kernel,
        out_shape=jax.ShapeDtypeStruct((2 * COLS // DEVS, COLS), F32),
        in_specs=[vmem],
        out_specs=vmem,
        scratch_shapes=[
            pltpu.VMEM((COLS, COLS), F32),
            pltpu.VMEM((COLS, COLS), F32),
            pltpu.VMEM((NB, NB), F32),
        ],
        compiler_params=pltpu.CompilerParams(vmem_limit_bytes=32 << 20),
        cost_estimate=pl.CostEstimate(flops=50_000_000_000, bytes_accessed=100_000_000, transcendentals=0),
        name="cholesky_rows",
    )(full)


def place_kernel(order_in, counts_in, arrived_a, arrived_b, sketch, order, counts, stage, zero, tab_sem, in_sem, sem):
    me = lax.axis_index("dev")
    tables = [
        pltpu.make_async_copy(order_in, order, tab_sem.at[0]),
        pltpu.make_async_copy(counts_in, counts, tab_sem.at[1]),
    ]
    for table in tables:
        table.start()
    zero[...] = jnp.zeros_like(zero)
    for table in tables:
        table.wait()

    def add(e, c):
        return c + jnp.where(e < me, counts[0, e], 0)

    offset = lax.fori_loop(0, DEVS, add, jnp.int32(0))
    held = counts[0, me]

    def load(j):
        source = order[0, jnp.minimum(offset + j, POSITIONS - 1)] >> 4
        return (
            pltpu.make_async_copy(arrived_a.at[source], stage.at[j, pl.ds(0, EARLY)], in_sem.at[j, 0]),
            pltpu.make_async_copy(arrived_b.at[source], stage.at[j, pl.ds(EARLY, KEEP - EARLY)], in_sem.at[j, 1]),
        )

    def start(j, c):
        @pl.when(j < held)
        def _():
            for part in load(j):
                part.start()

        @pl.when(j >= held)
        def _():
            pltpu.make_async_copy(zero, sketch.at[j], sem.at[j]).start()

        return c

    def store(j, c):
        @pl.when(j < held)
        def _():
            for part in load(j):
                part.wait()
            pltpu.make_async_copy(stage.at[j], sketch.at[j], sem.at[j]).start()

        return c

    def wait(j, c):
        pltpu.make_async_copy(zero, sketch.at[j], sem.at[j]).wait()
        return c

    lax.fori_loop(0, DEVS, start, 0)
    lax.fori_loop(0, DEVS, store, 0)
    lax.fori_loop(0, DEVS, wait, 0)


def place(block_order, counts, arrived_a, arrived_b):
    hbm = pl.BlockSpec(memory_space=pltpu.HBM)
    return pl.pallas_call(
        place_kernel,
        out_shape=jax.ShapeDtypeStruct((DEVS, KEEP, COLS), F32),
        in_specs=[hbm] * 4,
        out_specs=hbm,
        scratch_shapes=[
            pltpu.SMEM((1, POSITIONS), I32),
            pltpu.SMEM((1, DEVS), I32),
            pltpu.VMEM((DEVS, KEEP, COLS), F32),
            pltpu.VMEM((KEEP, COLS), F32),
            pltpu.SemaphoreType.DMA((2,)),
            pltpu.SemaphoreType.DMA((DEVS, 2)),
            pltpu.SemaphoreType.DMA((DEVS,)),
        ],
        compiler_params=pltpu.CompilerParams(vmem_limit_bytes=62 << 20),
        name="place_slots",
    )(block_order, counts, arrived_a, arrived_b)


def body(matrix, block_order, counts, sign_bits, row_mask):
    early, late, gram = mix(matrix, block_order, counts, sign_bits, row_mask)
    full, early = reduce_gram(gram, early)
    late, full = lax.optimization_barrier((late, full))
    late = lax.all_to_all(late, "dev", split_axis=0, concat_axis=0, tiled=True)
    rows = cholesky_rows(full)
    half = rows.shape[0] // 2
    first = lax.rem(lax.axis_index("dev"), 2) == 0
    mine = jnp.where(first, rows[:half], rows[half:])
    other = jnp.where(first, rows[half:], rows[:half])
    other = lax.ppermute(other, "dev", [(d, d ^ 1) for d in range(DEVS)])
    sketch = place(block_order, counts, early, late)
    group_factor = jnp.where(first, mine, other)[None]
    factor = jnp.where(first, other, mine)
    return sketch.reshape(DEVS * KEEP, COLS), group_factor, factor


def solution(mesh):
    placed = (
        P(("grp", "dev"), None),
        P("grp", None),
        P("grp", None),
        P("grp", None, None),
        P("grp", None, None),
    )
    return jax.shard_map(
        body,
        mesh=mesh,
        in_specs=placed,
        out_specs=(P(("grp", "dev"), None), P("grp", "dev", None), P("dev", None)),
        check_vma=False,
    )
```

```python
import jax
import jax.numpy as jnp
from jax import lax
from jax.experimental import pallas as pl
from jax.experimental.pallas import tpu as pltpu
from jax.sharding import PartitionSpec as P

MESH = pl.DeviceIdType.MESH
F32, BF16, I32 = jnp.float32, jnp.bfloat16, jnp.int32
BLOCK = 128
KEEP = 32
NB = 128
COLS = 1024
NBLK = COLS // NB
PER = 16
POSITIONS = 512
DEVS = 32
GRPS = 8
CHIPS = 16
SHARD = NBLK * (NBLK + 1) // 2 * NB // DEVS
ZROWS = 24
HALF = SHARD // 2
CUT = 40
EARLY = 8

OTHERS = [
    (x, y, c)
    for c in range(2)
    for x, y in ((1, 0), (0, 1), (3, 0), (0, 3), (1, 1), (3, 3), (1, 3), (3, 1), (2, 0), (0, 2), (2, 1), (1, 2), (2, 3), (3, 2), (2, 2))
] + [(0, 0, 1)]
GAPS = (1, 0, 0, 12, 11)


def packed(i, j):
    return i * NBLK - i * (i - 1) // 2 + (j - i)


def pieces(block):
    row = 0
    while row < NB:
        shard, start = divmod(block * NB + row, HALF)
        size = min(HALF - start, NB - row)
        yield row, size, (shard // 32, shard // 16 % 2, shard // 4 % 4, shard % 4), start
        row += size


def split2(x):
    h = x.astype(BF16)
    return h, (x - h.astype(F32)).astype(BF16)


def dot_t(a, b):
    return lax.dot_general(a, b, (((0,), (0,)), ((), ())), preferred_element_type=F32)


def dot_n(a, b):
    return lax.dot_general(a, b, (((1,), (0,)), ((), ())), preferred_element_type=F32)


def mix_kernel(order_in, counts_in, matrix, sign_bits, row_mask, send_a, send_b, kept, x, order, counts, signs, masks, s_rows, owner_v, place, tab_sem, in_sem, out_sem):
    me = lax.axis_index("dev")

    def fetch(k):
        return pltpu.make_async_copy(
            matrix.at[pl.ds(k * BLOCK, BLOCK)], x.at[pl.ds(k * BLOCK, BLOCK)], in_sem.at[k]
        )

    pairs = ((order_in, order), (counts_in, counts), (sign_bits, signs), (row_mask, masks))
    tables = [pltpu.make_async_copy(a, b, tab_sem.at[i]) for i, (a, b) in enumerate(pairs)]
    for table in tables:
        table.start()
    for k in range(PER):
        fetch(k).start()
    tables[0].wait()
    tables[1].wait()

    block = lax.broadcasted_iota(I32, (PER, POSITIONS), 0) + me * PER
    hit = jnp.where(order[...] == block, 1.0, 0.0)
    where = lax.broadcasted_iota(I32, (PER, POSITIONS), 1).astype(F32)
    pos = jnp.sum(hit * where, axis=1, keepdims=True)
    earlier = lax.broadcasted_iota(I32, (DEVS, DEVS), 0) <= lax.broadcasted_iota(I32, (DEVS, DEVS), 1)
    held = jnp.broadcast_to(counts[...].astype(F32), (PER, DEVS))
    ends = dot_n(held.astype(BF16), jnp.where(earlier, 1.0, 0.0).astype(BF16))
    owner = jnp.sum(jnp.where(ends <= pos, 1.0, 0.0), axis=1, keepdims=True)
    owner_v[...] = jnp.broadcast_to(owner, (PER, BLOCK)).astype(I32)
    owned = pltpu.make_async_copy(owner_v, place, tab_sem.at[4])
    owned.start()

    row = lax.broadcasted_iota(I32, (BLOCK, BLOCK), 0)
    col = lax.broadcasted_iota(I32, (BLOCK, BLOCK), 1)
    parity = row & col
    for shift in (4, 2, 1):
        parity = parity ^ (parity >> shift)
    walsh = (1 - 2 * (parity & 1)).astype(F32).astype(BF16)
    upto = jnp.where(row <= col, 1.0, 0.0).astype(BF16)
    tables[2].wait()
    tables[3].wait()
    table = jnp.concatenate([masks[0], signs[0]], axis=1).astype(F32).astype(BF16)
    both = dot_n(hit.astype(BF16), table)
    mask = both[:, :BLOCK]
    sign = 1.0 - 2.0 * both[:, BLOCK:]
    running = dot_n(mask.astype(BF16), upto).astype(I32)
    nth = lax.broadcasted_iota(I32, (KEEP, BLOCK), 0) + 1
    chosen = [
        jnp.where((running[k : k + 1] == nth) & (mask[k : k + 1] > 0.5), 1.0, 0.0) for k in range(PER)
    ]
    mixing = dot_n(jnp.concatenate(chosen, axis=0).astype(BF16), walsh)

    outs = []
    for k in range(PER):
        t = (mixing[k * KEEP : (k + 1) * KEEP] * sign[k : k + 1]).astype(BF16)
        fetch(k).wait()
        block = x[k * BLOCK : (k + 1) * BLOCK, :]
        hi = block.astype(BF16)
        rest = block - hi.astype(F32)
        mixed = dot_n(t, hi) + dot_n(t, rest.astype(BF16))
        mixed = mixed * float(BLOCK) ** -0.5
        rows = slice(k * KEEP, (k + 1) * KEEP)
        s_rows[rows, :] = mixed
        out = pltpu.make_async_copy(s_rows.at[pl.ds(k * KEEP, KEEP)], kept.at[pl.ds(k * KEEP, KEEP)], out_sem.at[k, 2])
        out.start()
        outs.append(out)
        if k == 0:
            owned.wait()
        cut = k * KEEP + EARLY
        for i, part, send in ((0, pl.ds(k * KEEP, EARLY), send_a), (1, pl.ds(cut, KEEP - EARLY), send_b)):
            out = pltpu.make_async_copy(s_rows.at[part], send.at[place[k, 0]], out_sem.at[k, i])
            out.start()
            outs.append(out)

    for out in outs:
        out.wait()


def mix(matrix, block_order, counts, sign_bits, row_mask):
    hbm = pl.BlockSpec(memory_space=pltpu.HBM)
    rows = PER * KEEP
    return pl.pallas_call(
        mix_kernel,
        out_shape=(
            jax.ShapeDtypeStruct((DEVS, EARLY, COLS), F32),
            jax.ShapeDtypeStruct((DEVS, KEEP - EARLY, COLS), F32),
            jax.ShapeDtypeStruct((rows, COLS), F32),
        ),
        in_specs=[hbm] * 5,
        out_specs=(hbm, hbm, hbm),
        scratch_shapes=[
            pltpu.VMEM((PER * BLOCK, COLS), F32),
            pltpu.VMEM((1, POSITIONS), I32),
            pltpu.VMEM((1, DEVS), I32),
            pltpu.VMEM((1, POSITIONS, BLOCK), I32),
            pltpu.VMEM((1, POSITIONS, BLOCK), I32),
            pltpu.VMEM((rows, COLS), F32),
            pltpu.VMEM((PER, BLOCK), I32),
            pltpu.SMEM((PER, BLOCK), I32),
            pltpu.SemaphoreType.DMA((5,)),
            pltpu.SemaphoreType.DMA((PER,)),
            pltpu.SemaphoreType.DMA((PER, 3)),
        ],
        compiler_params=pltpu.CompilerParams(vmem_limit_bytes=62 << 20),
        name="mix_rows",
    )(block_order, counts, matrix, sign_bits, row_mask)


def reduce_kernel(
    kept, blocks, full, arrived, rows, s_hi, s_mid, g, acc, fwd, got, fwd_p, fwd_m, got2, own, z_buf, z_sum, z_all, mean,
    own_sem, pair_sem, rs_sem, z_sem, m_sem, swap_sem, ag_sem, all_sem, stay_sem,
):
    grp = lax.axis_index("grp")
    dev = lax.axis_index("dev")
    core = lax.rem(dev, 2)
    chip = dev // 2
    cx, cy = chip // 4, lax.rem(chip, 4)
    partner = chip * 2 + 1 - core
    first = (cx, cy)
    second = (cy, cx)

    def mod4(i):
        return lax.rem(i + 4, 4)

    def at_offset(dx, dy, flip=0):
        return (mod4(cx + dx) * 4 + mod4(cy + dy)) * 2 + lax.rem(core + flip, 2)

    def neighbour(h, dim, step):
        return at_offset(step, 0) if (h + dim) % 2 == 0 else at_offset(0, step)

    def copy(src, dst, sem, at, to_dev, to_grp=grp):
        return pltpu.make_async_remote_copy(
            src_ref=src,
            dst_ref=dst,
            send_sem=sem.at[(0, *at)],
            recv_sem=sem.at[(1, *at)],
            device_id=(to_grp, to_dev),
            device_id_type=MESH,
        )

    sent = []

    def send(*args):
        c = copy(*args)
        c.start()
        sent.append(c)

    def receive(dst, sem, at):
        copy(dst, dst, sem, at, partner).wait_recv()

    def z_start(z):
        return pl.multiple_of((z * 15) // 7 * 8, 8)

    def run(lo, hi, act):
        def step(d, c):
            act(d)
            return c

        lax.fori_loop(lo, hi, step, 0)

    keep = pltpu.make_async_copy(kept, rows, own_sem)
    keep.start()
    barrier = pltpu.get_barrier_semaphore()

    def greet(to_dev, to_grp=grp):
        pl.semaphore_signal(barrier, inc=1, device_id=(to_grp, to_dev), device_id_type=MESH)

    for others in OTHERS:
        greet(at_offset(*others))
    run(1, GRPS, lambda d: greet(dev, lax.rem(grp + d, GRPS)))

    def block_copy(i):
        to = at_offset(*OTHERS[i])
        return copy(blocks.at[to], arrived.at[dev], all_sem, (i,), to)

    pending = list(range(len(OTHERS)))

    def fill(count):
        for _ in range(min(count, len(pending))):
            block_copy(pending.pop(0)).start()

    keep.wait()
    hi, mid = split2(rows[...])
    s_hi[...] = hi
    s_mid[...] = mid
    steps = (2, 1, -1, 0)

    def pair_copy(h, a):
        return copy(g.at[1 - core, h, a], acc.at[h, a], pair_sem, (h, a), partner)

    stay = pltpu.make_async_copy(blocks.at[dev], arrived.at[dev], stay_sem)
    stay.start()
    gone = 0
    for i in range(NBLK):
        left = slice(i * NB, (i + 1) * NB)
        band = dot_t(s_hi[:, left], s_hi[:, i * NB :]) + dot_t(s_hi[:, left], s_mid[:, i * NB :])
        band = band + dot_t(s_mid[:, left], s_hi[:, i * NB :])
        for j in range(i, NBLK):
            for row, size, (core_, half, x, y), start in pieces(packed(i, j)):
                part = band[row : row + size, (j - i) * NB : (j - i + 1) * NB]
                g[core_, half, x, y, start : start + size, :] = part
        if i == 0:
            pl.semaphore_wait(barrier, len(OTHERS) + GRPS - 1)
        while gone < 16 and (gone + 1) * 4 * HALF <= (packed(i, NBLK - 1) + 1) * NB:
            core_, half, x = gone // 8, gone // 4 % 2, gone % 4

            @pl.when(core != core_)
            def _():
                pair_copy(half, x).start()

            gone += 1
        fill(GAPS[0])

    def pair_sum(i):
        for h in range(2):
            a = mod4(first[h] + steps[i])
            receive(acc.at[h, a], pair_sem, (h, a))
            acc[h, a] = acc[h, a] + g[core, h, a]

    lo, hi = pl.ds(0, 2), pl.ds(2, 2)
    pair_sum(0)
    for h in range(2):
        u = first[h]
        send(acc.at[h, mod4(u + 2), lo], fwd.at[h, 0], rs_sem, (h, 0), neighbour(h, 0, 1))
        send(acc.at[h, mod4(u + 2), hi], fwd.at[h, 1], rs_sem, (h, 1), neighbour(h, 0, -1))
    pair_sum(1)
    for h in range(2):
        send(acc.at[h, mod4(first[h] + 1), hi], got.at[h, 0, hi], rs_sem, (h, 2), neighbour(h, 0, 1))
    pair_sum(2)
    for h in range(2):
        send(acc.at[h, mod4(first[h] - 1), lo], got.at[h, 1, lo], rs_sem, (h, 3), neighbour(h, 0, -1))
    pair_sum(3)
    for h in range(2):
        up, down = mod4(first[h] + 1), mod4(first[h] - 1)
        receive(fwd.at[h, 0], rs_sem, (h, 0))
        acc[h, up, 0:2] = acc[h, up, 0:2] + fwd[h, 0]
        send(acc.at[h, up, lo], got.at[h, 0, lo], rs_sem, (h, 4), neighbour(h, 0, 1))
        receive(fwd.at[h, 1], rs_sem, (h, 1))
        acc[h, down, 2:4] = acc[h, down, 2:4] + fwd[h, 1]
        send(acc.at[h, down, hi], got.at[h, 1, hi], rs_sem, (h, 5), neighbour(h, 0, -1))
    fill(GAPS[1])
    top, bottom = pl.ds(0, CUT), pl.ds(CUT, HALF - CUT)
    for h in range(2):
        u, v = first[h], second[h]
        receive(got.at[h, 0, hi], rs_sem, (h, 2))
        receive(got.at[h, 1, lo], rs_sem, (h, 3))
        receive(got.at[h, 0, lo], rs_sem, (h, 4))
        receive(got.at[h, 1, hi], rs_sem, (h, 5))
        acc[h, u] = acc[h, u] + got[h, 0] + got[h, 1]
        send(acc.at[h, u, mod4(v + 2), top], fwd_p.at[h], rs_sem, (h, 6), neighbour(h, 1, 1))
        send(acc.at[h, u, mod4(v + 2), bottom], fwd_m.at[h], rs_sem, (h, 7), neighbour(h, 1, -1))
        send(acc.at[h, u, mod4(v + 1), bottom], got2.at[h, 0, bottom], rs_sem, (h, 8), neighbour(h, 1, 1))
        send(acc.at[h, u, mod4(v - 1), top], got2.at[h, 1, top], rs_sem, (h, 9), neighbour(h, 1, -1))
    for h in range(2):
        u, up, down = first[h], mod4(second[h] + 1), mod4(second[h] - 1)
        receive(fwd_p.at[h], rs_sem, (h, 6))
        acc[h, u, up, 0:CUT] = acc[h, u, up, 0:CUT] + fwd_p[h]
        send(acc.at[h, u, up, top], got2.at[h, 0, top], rs_sem, (h, 10), neighbour(h, 1, 1))
        receive(fwd_m.at[h], rs_sem, (h, 7))
        acc[h, u, down, CUT:HALF] = acc[h, u, down, CUT:HALF] + fwd_m[h]
        send(acc.at[h, u, down, bottom], got2.at[h, 1, bottom], rs_sem, (h, 11), neighbour(h, 1, -1))
    fill(GAPS[2])
    for h in range(2):
        receive(got2.at[h, 0, bottom], rs_sem, (h, 8))
        receive(got2.at[h, 1, top], rs_sem, (h, 9))
        receive(got2.at[h, 0, top], rs_sem, (h, 10))
        receive(got2.at[h, 1, bottom], rs_sem, (h, 11))
        total = acc[h, first[h], second[h]] + got2[h, 0] + got2[h, 1]
        own[h * HALF : (h + 1) * HALF, :] = total * (1.0 / (POSITIONS * KEEP))

    def z_copy(d):
        to = lax.rem(grp + d, GRPS)
        return copy(own.at[pl.ds(z_start(to), ZROWS)], z_buf.at[d], z_sem, (d,), dev, to)

    run(1, GRPS, lambda d: z_copy(d).start())

    def block(h):
        return full.at[h, first[h], second[h], core]

    def swap(src, h):
        return copy(src.at[pl.ds(h * HALF, HALF)], block(h), swap_sem, (h,), partner)

    def spreads(i, h):
        def at(i, j):
            return full.at[h, mod4(first[h] + i), mod4(second[h] + j)]

        def both(piece, slot, dim):
            return [(piece, slot, dim, 1), (piece, slot + 1, dim, -1)]

        def on(before, after, slot, dim):
            return [(before.at[0], slot + 2, dim, 1), (after.at[1], slot + 3, dim, -1)]

        if i == 0:
            return both(at(0, 0), 0, 1) + both(at(0, 0), 4, 0)
        if i == 1:
            return on(at(0, -1), at(0, 1), 0, 1) + both(at(0, -1), 8, 0) + both(at(0, 1), 12, 0)
        if i == 2:
            return on(at(-1, 0), at(1, 0), 4, 0) + both(at(0, 2), 16, 0)
        return [x for j, slot in ((-1, 8), (1, 12), (2, 16)) for x in on(at(-1, j), at(1, j), slot, 0)]

    def needs(i, h):
        def at(i, j):
            return full.at[h, mod4(first[h] + i), mod4(second[h] + j)]

        if i == 0:
            return []
        if i == 1:
            return [(at(0, -1), 0), (at(0, 1), 1)]
        if i == 2:
            return [(at(-1, 0), 4), (at(1, 0), 5), (at(0, 2).at[0], 2), (at(0, 2).at[1], 3)]
        if i == 3:
            return [x for j, slot in ((-1, 8), (1, 12), (2, 16)) for x in ((at(-1, j), slot), (at(1, j), slot + 1))]
        return [
            x
            for j, slot in ((0, 4), (-1, 8), (1, 12), (2, 16))
            for x in ((at(2, j).at[0], slot + 2), (at(2, j).at[1], slot + 3))
        ]

    def leave(piece, slot, h, dim, step):
        return copy(piece, piece, ag_sem, (h, slot), neighbour(h, dim, step))

    def stage(i):
        for h in range(2):
            for piece, slot in needs(i, h):
                receive(piece, ag_sem, (h, slot))
            if i < 4:
                for piece, slot, dim, step in spreads(i, h):
                    leave(piece, slot, h, dim, step).start()

    def begin(src):
        for h in range(2):
            full[h, first[h], second[h], core] = src[h * HALF : (h + 1) * HALF, :]
        for h in range(2):
            receive(full.at[h, first[h], second[h], 1 - core], swap_sem, (h,))
        stage(0)

    @pl.when(core == 1)
    def _():
        for h in range(2):
            swap(own, h).start()

    fill(GAPS[3])

    @pl.when(core == 0)
    def _():
        begin(own)

    run(1, GRPS, lambda d: z_copy(d).wait())
    total = own[pl.ds(z_start(grp), ZROWS), :]
    for d in range(1, GRPS):
        total = total + z_buf[d]
    z_sum[...] = total * (1.0 / GRPS)

    def m_copy(d):
        return copy(z_sum, z_all.at[grp], m_sem, (d,), dev, lax.rem(grp + d, GRPS))

    run(1, GRPS, lambda d: m_copy(d).start())
    z_all[grp] = z_sum[...]
    fill(GAPS[4])

    @pl.when(core == 0)
    def _():
        stage(1)

    def m_receive(d):
        receive(z_all.at[lax.rem(grp + GRPS - d, GRPS)], m_sem, (d,))

    run(1, GRPS, m_receive)
    for z in range(GRPS):
        start = (z * 15) // 7 * 8
        mean[start : start + ZROWS, :] = z_all[z]

    @pl.when(core == 0)
    def _():
        for h in range(2):
            swap(mean, h).start()

    @pl.when(core == 1)
    def _():
        begin(mean)
        stage(1)

    fill(len(OTHERS))
    stage(2)
    stage(3)
    stage(4)

    run(1, GRPS, lambda d: m_copy(d).wait_send())
    for h in range(2):
        swap(own, h).wait_send()
        for i in range(4):
            for piece, slot, dim, step in spreads(i, h):
                leave(piece, slot, h, dim, step).wait_send()
    for c in sent:
        c.wait_send()
    for h in range(2):
        for a in range(4):
            pair_copy(h, a).wait_send()
    for i in range(len(OTHERS)):
        dx, dy, flip = OTHERS[i]
        copy(blocks.at[dev], arrived.at[at_offset(-dx, -dy, flip)], all_sem, (i,), partner).wait_recv()
        block_copy(i).wait_send()
    stay.wait()


def reduce_gram(kept, blocks):
    dma = pltpu.SemaphoreType.DMA
    vmem = lambda *shape: pltpu.VMEM((*shape, NB), F32)
    return pl.pallas_call(
        reduce_kernel,
        out_shape=(
            jax.ShapeDtypeStruct((2, 4, 4, 2, HALF, NB), F32),
            jax.ShapeDtypeStruct(blocks.shape, F32),
        ),
        in_specs=[pl.BlockSpec(memory_space=pltpu.HBM)] * 2,
        out_specs=(pl.BlockSpec(memory_space=pltpu.VMEM), pl.BlockSpec(memory_space=pltpu.HBM)),
        scratch_shapes=[
            pltpu.VMEM(kept.shape, F32),
            pltpu.VMEM(kept.shape, BF16),
            pltpu.VMEM(kept.shape, BF16),
            vmem(2, 2, 4, 4, HALF),
            vmem(2, 4, 4, HALF),
            vmem(2, 2, 2, HALF),
            vmem(2, 2, 4, HALF),
            vmem(2, CUT),
            vmem(2, HALF - CUT),
            vmem(2, 2, HALF),
            vmem(SHARD),
            vmem(GRPS, ZROWS),
            vmem(ZROWS),
            vmem(GRPS, ZROWS),
            vmem(SHARD),
            dma,
            dma((2, 2, 4)),
            dma((2, 2, 12)),
            dma((2, GRPS)),
            dma((2, GRPS)),
            dma((2, 2)),
            dma((2, 2, 20)),
            dma((2, len(OTHERS))),
            dma,
        ],
        compiler_params=pltpu.CompilerParams(
            collective_id=0, has_side_effects=True, vmem_limit_bytes=61 << 20
        ),
        name="reduce_gram",
    )(kept, blocks)


def diag_factor(d):
    n = NB // 8
    lane = lax.broadcasted_iota(I32, (8, NB), 1)
    sub = lax.broadcasted_iota(I32, (8, NB), 0)

    def column(x, i):
        return jnp.broadcast_to(x[:, i : i + 1], (8, NB))

    def line(x, i):
        return jnp.broadcast_to(x[i : i + 1, :], (8, NB))

    t_rows = [d[8 * s : 8 * s + 8, :] for s in range(n)]
    e_rows = [jnp.where(lane == sub + 8 * s, 1.0, 0.0).astype(F32) for s in range(n)]
    r_out, e_out = [], []
    low, scale, r_lines, e_lines = {}, [], [], []
    for s in range(n):
        c0 = 8 * s
        t, e = t_rows[s], e_rows[s]
        cols = [column(t, c0 + j) for j in range(8)]
        if s:
            before = []
            for j in range(8):
                c = column(t_rows[s], c0 - 8 + j)
                for m in range(j):
                    c = c - before[m] * low[m, j]
                before.append(c * scale[j])
            for j in range(8):
                c = before[j]
                t = t - c * r_lines[j]
                e = e - c * e_lines[j]
                cols = [x - c * line(c, k) for k, x in enumerate(cols)]
        b = {(i, j): line(cols[j], i) for i in range(8) for j in range(i, 8)}
        rows = [line(t, j) for j in range(8)]
        extra = [line(e, j) for j in range(8)]
        low, scale, r_lines, e_lines = {}, [], [], []
        r_strip = e_strip = None
        for j in range(8):
            q = lax.rsqrt(b[j, j])
            scale.append(q)
            for k in range(j + 1, 8):
                low[j, k] = b[j, k] * q
            for i in range(j + 1, 8):
                for k in range(i, 8):
                    b[i, k] = b[i, k] - low[j, i] * low[j, k]
            rj, ej = rows[j] * q, extra[j] * q
            r_lines.append(rj)
            e_lines.append(ej)
            for i in range(j + 1, 8):
                rows[i] = rows[i] - low[j, i] * rj
                extra[i] = extra[i] - low[j, i] * ej
            r_strip = rj if j == 0 else jnp.where(sub == j, rj, r_strip)
            e_strip = ej if j == 0 else jnp.where(sub == j, ej, e_strip)
        r_out.append(r_strip)
        e_out.append(e_strip)
        if s + 2 >= n:
            continue
        w = jnp.concatenate([r_strip, e_strip], axis=1)
        h = w.astype(BF16).astype(F32)
        rest = w - h
        m = rest.astype(BF16).astype(F32)
        q = rest - m
        lhs = jnp.concatenate([v[:, :NB] for v in (h, h, m, m, h, q)], axis=0).astype(BF16)
        rhs = jnp.concatenate([h, m, h, m, q, h], axis=0).astype(BF16)
        update = dot_t(lhs, rhs)
        for i in range(s + 2, n):
            t_rows[i] = t_rows[i] - update[8 * i : 8 * i + 8, :NB]
            e_rows[i] = e_rows[i] - update[8 * i : 8 * i + 8, NB:]
    return jnp.concatenate(r_out, axis=0), jnp.concatenate(e_out, axis=0)


def cholesky_kernel(g, out, a, r, d):
    for i in range(NBLK):
        for j in range(i, NBLK):
            for row, size, (core_, half, x, y), start in pieces(packed(i, j)):
                part = g[half, x, y, core_, start : start + size, :]
                a[i * NB + row : i * NB + row + size, j * NB : (j + 1) * NB] = part
    row = lax.broadcasted_iota(I32, (NB, NB), 0)
    col = lax.broadcasted_iota(I32, (NB, NB), 1)
    d[...] = a[0:NB, 0:NB]

    def step(k, c):
        top, inverse = diag_factor(d[...])
        d[...] = jnp.where(row <= col, top, 0.0)
        hi, mid = split2(inverse)
        left = jnp.concatenate([hi, hi, mid], axis=1)
        for kk in range(NBLK):

            @pl.when(k == kk)
            def _():
                k0, k1 = kk * NB, (kk + 1) * NB
                r[k0:k1, k0:k1] = d[...]
                if kk:
                    r[k0:k1, 0:k0] = jnp.zeros((NB, k0), F32)
                if kk == NBLK - 1:
                    return
                hi, mid = split2(a[k0:k1, k1:])
                strip = dot_n(left, jnp.concatenate([hi, mid, hi], axis=0))
                r[k0:k1, k1:] = strip
                hi, mid = split2(strip)
                lhs = jnp.concatenate([hi, hi, mid], axis=0)
                rhs = jnp.concatenate([hi, mid, hi], axis=0)
                d[...] = a[k1 : k1 + NB, k1 : k1 + NB] - dot_t(lhs[:, :NB], rhs[:, :NB])
                for i in range((COLS - k1) // NB):
                    lo, hi_ = i * NB, (i + 1) * NB
                    if i:
                        a[k1 + lo : k1 + hi_, k1 + lo :] -= dot_t(lhs[:, lo:hi_], rhs[:, lo:])
                    elif kk < NBLK - 2:
                        a[k1 : k1 + NB, k1 + NB :] -= dot_t(lhs[:, :NB], rhs[:, NB:])

        return c

    lax.fori_loop(0, NBLK, step, 0)
    chip = lax.axis_index("dev") // 2
    out[...] = r[pl.ds(pl.multiple_of(chip * 64, 64), 64), :]


def cholesky_rows(full):
    vmem = pl.BlockSpec(memory_space=pltpu.VMEM)
    return pl.pallas_call(
        cholesky_kernel,
        out_shape=jax.ShapeDtypeStruct((2 * COLS // DEVS, COLS), F32),
        in_specs=[vmem],
        out_specs=vmem,
        scratch_shapes=[
            pltpu.VMEM((COLS, COLS), F32),
            pltpu.VMEM((COLS, COLS), F32),
            pltpu.VMEM((NB, NB), F32),
        ],
        compiler_params=pltpu.CompilerParams(vmem_limit_bytes=32 << 20),
        cost_estimate=pl.CostEstimate(flops=50_000_000_000, bytes_accessed=100_000_000, transcendentals=0),
        name="cholesky_rows",
    )(full)


def place_kernel(order_in, counts_in, arrived_a, arrived_b, sketch, order, counts, stage, zero, tab_sem, in_sem, sem):
    me = lax.axis_index("dev")
    tables = [
        pltpu.make_async_copy(order_in, order, tab_sem.at[0]),
        pltpu.make_async_copy(counts_in, counts, tab_sem.at[1]),
    ]
    for table in tables:
        table.start()
    zero[...] = jnp.zeros_like(zero)
    for table in tables:
        table.wait()

    def add(e, c):
        return c + jnp.where(e < me, counts[0, e], 0)

    offset = lax.fori_loop(0, DEVS, add, jnp.int32(0))
    held = counts[0, me]

    def load(j):
        source = order[0, jnp.minimum(offset + j, POSITIONS - 1)] >> 4
        return (
            pltpu.make_async_copy(arrived_a.at[source], stage.at[j, pl.ds(0, EARLY)], in_sem.at[j, 0]),
            pltpu.make_async_copy(arrived_b.at[source], stage.at[j, pl.ds(EARLY, KEEP - EARLY)], in_sem.at[j, 1]),
        )

    def start(j, c):
        @pl.when(j < held)
        def _():
            for part in load(j):
                part.start()

        @pl.when(j >= held)
        def _():
            pltpu.make_async_copy(zero, sketch.at[j], sem.at[j]).start()

        return c

    def store(j, c):
        @pl.when(j < held)
        def _():
            for part in load(j):
                part.wait()
            pltpu.make_async_copy(stage.at[j], sketch.at[j], sem.at[j]).start()

        return c

    def wait(j, c):
        pltpu.make_async_copy(zero, sketch.at[j], sem.at[j]).wait()
        return c

    lax.fori_loop(0, DEVS, start, 0)
    lax.fori_loop(0, DEVS, store, 0)
    lax.fori_loop(0, DEVS, wait, 0)


def place(block_order, counts, arrived_a, arrived_b):
    hbm = pl.BlockSpec(memory_space=pltpu.HBM)
    return pl.pallas_call(
        place_kernel,
        out_shape=jax.ShapeDtypeStruct((DEVS, KEEP, COLS), F32),
        in_specs=[hbm] * 4,
        out_specs=hbm,
        scratch_shapes=[
            pltpu.SMEM((1, POSITIONS), I32),
            pltpu.SMEM((1, DEVS), I32),
            pltpu.VMEM((DEVS, KEEP, COLS), F32),
            pltpu.VMEM((KEEP, COLS), F32),
            pltpu.SemaphoreType.DMA((2,)),
            pltpu.SemaphoreType.DMA((DEVS, 2)),
            pltpu.SemaphoreType.DMA((DEVS,)),
        ],
        compiler_params=pltpu.CompilerParams(vmem_limit_bytes=62 << 20),
        name="place_slots",
    )(block_order, counts, arrived_a, arrived_b)


def body(matrix, block_order, counts, sign_bits, row_mask):
    early, late, kept = mix(matrix, block_order, counts, sign_bits, row_mask)
    full, early = reduce_gram(kept, early)
    late, full = lax.optimization_barrier((late, full))
    late = lax.all_to_all(late, "dev", split_axis=0, concat_axis=0, tiled=True)
    rows = cholesky_rows(full)
    half = rows.shape[0] // 2
    first = lax.rem(lax.axis_index("dev"), 2) == 0
    mine = jnp.where(first, rows[:half], rows[half:])
    other = jnp.where(first, rows[half:], rows[:half])
    other = lax.ppermute(other, "dev", [(d, d ^ 1) for d in range(DEVS)])
    sketch = place(block_order, counts, early, late)
    group_factor = jnp.where(first, mine, other)[None]
    factor = jnp.where(first, other, mine)
    return sketch.reshape(DEVS * KEEP, COLS), group_factor, factor


def solution(mesh):
    placed = (
        P(("grp", "dev"), None),
        P("grp", None),
        P("grp", None),
        P("grp", None, None),
        P("grp", None, None),
    )
    return jax.shard_map(
        body,
        mesh=mesh,
        in_specs=placed,
        out_specs=(P(("grp", "dev"), None), P("grp", "dev", None), P("dev", None)),
        check_vma=False,
    )
```

```python
import jax
import jax.numpy as jnp
from jax import lax
from jax.experimental import pallas as pl
from jax.experimental.pallas import tpu as pltpu
from jax.sharding import PartitionSpec as P

MESH = pl.DeviceIdType.MESH
F32, BF16, I32 = jnp.float32, jnp.bfloat16, jnp.int32
BLOCK = 128
KEEP = 32
NB = 128
COLS = 1024
NBLK = COLS // NB
PER = 16
POSITIONS = 512
DEVS = 32
GRPS = 8
CHIPS = 16
SHARD = NBLK * (NBLK + 1) // 2 * NB // DEVS
ZROWS = 24
HALF = SHARD // 2
CUT = 40
EARLY = 8

OTHERS = [
    (x, y, c)
    for c in range(2)
    for x, y in ((1, 0), (0, 1), (3, 0), (0, 3), (1, 1), (3, 3), (1, 3), (3, 1), (2, 0), (0, 2), (2, 1), (1, 2), (2, 3), (3, 2), (2, 2))
] + [(0, 0, 1)]
GAPS = (1, 0, 0, 12, 11)


def packed(i, j):
    return i * NBLK - i * (i - 1) // 2 + (j - i)


def pieces(block):
    row = 0
    while row < NB:
        shard, start = divmod(block * NB + row, HALF)
        size = min(HALF - start, NB - row)
        yield row, size, (shard // 32, shard // 16 % 2, shard // 4 % 4, shard % 4), start
        row += size


def split2(x):
    h = x.astype(BF16)
    return h, (x - h.astype(F32)).astype(BF16)


def dot_t(a, b):
    return lax.dot_general(a, b, (((0,), (0,)), ((), ())), preferred_element_type=F32)


def dot_n(a, b):
    return lax.dot_general(a, b, (((1,), (0,)), ((), ())), preferred_element_type=F32)


def mix_kernel(order_in, counts_in, matrix, sign_bits, row_mask, send_a, send_b, kept, x, order, counts, signs, masks, s_rows, owner_v, place, tab_sem, in_sem, out_sem):
    me = lax.axis_index("dev")

    def fetch(k):
        return pltpu.make_async_copy(
            matrix.at[pl.ds(k * BLOCK, BLOCK)], x.at[pl.ds(k * BLOCK, BLOCK)], in_sem.at[k]
        )

    pairs = ((order_in, order), (counts_in, counts), (sign_bits, signs), (row_mask, masks))
    tables = [pltpu.make_async_copy(a, b, tab_sem.at[i]) for i, (a, b) in enumerate(pairs)]
    for table in tables:
        table.start()
    for k in range(PER):
        fetch(k).start()
    tables[0].wait()
    tables[1].wait()

    block = lax.broadcasted_iota(I32, (PER, POSITIONS), 0) + me * PER
    hit = jnp.where(order[...] == block, 1.0, 0.0)
    where = lax.broadcasted_iota(I32, (PER, POSITIONS), 1).astype(F32)
    pos = jnp.sum(hit * where, axis=1, keepdims=True)
    earlier = lax.broadcasted_iota(I32, (DEVS, DEVS), 0) <= lax.broadcasted_iota(I32, (DEVS, DEVS), 1)
    held = jnp.broadcast_to(counts[...].astype(F32), (PER, DEVS))
    ends = dot_n(held.astype(BF16), jnp.where(earlier, 1.0, 0.0).astype(BF16))
    owner = jnp.sum(jnp.where(ends <= pos, 1.0, 0.0), axis=1, keepdims=True)
    owner_v[...] = jnp.broadcast_to(owner, (PER, BLOCK)).astype(I32)
    owned = pltpu.make_async_copy(owner_v, place, tab_sem.at[4])
    owned.start()

    row = lax.broadcasted_iota(I32, (BLOCK, BLOCK), 0)
    col = lax.broadcasted_iota(I32, (BLOCK, BLOCK), 1)
    parity = row & col
    for shift in (4, 2, 1):
        parity = parity ^ (parity >> shift)
    walsh = (1 - 2 * (parity & 1)).astype(F32).astype(BF16)
    upto = jnp.where(row <= col, 1.0, 0.0).astype(BF16)
    tables[2].wait()
    tables[3].wait()
    table = jnp.concatenate([masks[0], signs[0]], axis=1).astype(F32).astype(BF16)
    both = dot_n(hit.astype(BF16), table)
    mask = both[:, :BLOCK]
    sign = 1.0 - 2.0 * both[:, BLOCK:]
    running = dot_n(mask.astype(BF16), upto).astype(I32)
    nth = lax.broadcasted_iota(I32, (KEEP, BLOCK), 0) + 1
    chosen = [
        jnp.where((running[k : k + 1] == nth) & (mask[k : k + 1] > 0.5), 1.0, 0.0) for k in range(PER)
    ]
    mixing = dot_n(jnp.concatenate(chosen, axis=0).astype(BF16), walsh)

    outs = []
    for k in range(PER):
        t = (mixing[k * KEEP : (k + 1) * KEEP] * sign[k : k + 1]).astype(BF16)
        fetch(k).wait()
        block = x[k * BLOCK : (k + 1) * BLOCK, :]
        hi = block.astype(BF16)
        rest = block - hi.astype(F32)
        mixed = dot_n(t, hi) + dot_n(t, rest.astype(BF16))
        mixed = mixed * float(BLOCK) ** -0.5
        rows = slice(k * KEEP, (k + 1) * KEEP)
        s_rows[rows, :] = mixed
        out = pltpu.make_async_copy(s_rows.at[pl.ds(k * KEEP, KEEP)], kept.at[pl.ds(k * KEEP, KEEP)], out_sem.at[k, 2])
        out.start()
        outs.append(out)
        if k == 0:
            owned.wait()
        cut = k * KEEP + EARLY
        for i, part, send in ((0, pl.ds(k * KEEP, EARLY), send_a), (1, pl.ds(cut, KEEP - EARLY), send_b)):
            out = pltpu.make_async_copy(s_rows.at[part], send.at[place[k, 0]], out_sem.at[k, i])
            out.start()
            outs.append(out)

    for out in outs:
        out.wait()


def mix(matrix, block_order, counts, sign_bits, row_mask):
    hbm = pl.BlockSpec(memory_space=pltpu.HBM)
    rows = PER * KEEP
    return pl.pallas_call(
        mix_kernel,
        out_shape=(
            jax.ShapeDtypeStruct((DEVS, EARLY, COLS), F32),
            jax.ShapeDtypeStruct((DEVS, KEEP - EARLY, COLS), F32),
            jax.ShapeDtypeStruct((rows, COLS), F32),
        ),
        in_specs=[hbm] * 5,
        out_specs=(hbm, hbm, hbm),
        scratch_shapes=[
            pltpu.VMEM((PER * BLOCK, COLS), F32),
            pltpu.VMEM((1, POSITIONS), I32),
            pltpu.VMEM((1, DEVS), I32),
            pltpu.VMEM((1, POSITIONS, BLOCK), I32),
            pltpu.VMEM((1, POSITIONS, BLOCK), I32),
            pltpu.VMEM((rows, COLS), F32),
            pltpu.VMEM((PER, BLOCK), I32),
            pltpu.SMEM((PER, BLOCK), I32),
            pltpu.SemaphoreType.DMA((5,)),
            pltpu.SemaphoreType.DMA((PER,)),
            pltpu.SemaphoreType.DMA((PER, 3)),
        ],
        compiler_params=pltpu.CompilerParams(vmem_limit_bytes=62 << 20),
        name="mix_rows",
    )(block_order, counts, matrix, sign_bits, row_mask)


def reduce_kernel(
    kept, blocks, full, arrived, rows, s_hi, s_mid, g, acc, fwd, got, fwd_p, fwd_m, got2, own, z_buf, z_sum, z_all, mean,
    own_sem, pair_sem, rs_sem, z_sem, m_sem, swap_sem, ag_sem, all_sem, stay_sem,
):
    grp = lax.axis_index("grp")
    dev = lax.axis_index("dev")
    core = lax.rem(dev, 2)
    chip = dev // 2
    cx, cy = chip // 4, lax.rem(chip, 4)
    partner = chip * 2 + 1 - core
    first = (cx, cy)
    second = (cy, cx)

    def mod4(i):
        return lax.rem(i + 4, 4)

    def at_offset(dx, dy, flip=0):
        return (mod4(cx + dx) * 4 + mod4(cy + dy)) * 2 + lax.rem(core + flip, 2)

    def neighbour(h, dim, step):
        return at_offset(step, 0) if (h + dim) % 2 == 0 else at_offset(0, step)

    def copy(src, dst, sem, at, to_dev, to_grp=grp):
        return pltpu.make_async_remote_copy(
            src_ref=src,
            dst_ref=dst,
            send_sem=sem.at[(0, *at)],
            recv_sem=sem.at[(1, *at)],
            device_id=(to_grp, to_dev),
            device_id_type=MESH,
        )

    sent = []

    def send(*args):
        c = copy(*args)
        c.start()
        sent.append(c)

    def receive(dst, sem, at):
        copy(dst, dst, sem, at, partner).wait_recv()

    def z_start(z):
        return pl.multiple_of((z * 15) // 7 * 8, 8)

    def run(lo, hi, act):
        def step(d, c):
            act(d)
            return c

        lax.fori_loop(lo, hi, step, 0)

    keep = pltpu.make_async_copy(kept, rows, own_sem)
    keep.start()
    barrier = pltpu.get_barrier_semaphore()

    def greet(to_dev, to_grp=grp):
        pl.semaphore_signal(barrier, inc=1, device_id=(to_grp, to_dev), device_id_type=MESH)

    for others in OTHERS:
        greet(at_offset(*others))
    run(1, GRPS, lambda d: greet(dev, lax.rem(grp + d, GRPS)))

    def block_copy(i):
        to = at_offset(*OTHERS[i])
        return copy(blocks.at[to], arrived.at[dev], all_sem, (i,), to)

    pending = list(range(len(OTHERS)))

    def fill(count):
        for _ in range(min(count, len(pending))):
            block_copy(pending.pop(0)).start()

    keep.wait()
    hi, mid = split2(rows[...])
    s_hi[...] = hi
    s_mid[...] = mid
    steps = (2, 1, -1, 0)

    def pair_copy(h, a):
        return copy(g.at[1 - core, h, a], acc.at[h, a], pair_sem, (h, a), partner)

    stay = pltpu.make_async_copy(blocks.at[dev], arrived.at[dev], stay_sem)
    stay.start()
    gone = 0
    for i in range(NBLK):
        left = slice(i * NB, (i + 1) * NB)
        band = dot_t(s_hi[:, left], s_hi[:, i * NB :]) + dot_t(s_hi[:, left], s_mid[:, i * NB :])
        band = band + dot_t(s_mid[:, left], s_hi[:, i * NB :])
        for j in range(i, NBLK):
            for row, size, (core_, half, x, y), start in pieces(packed(i, j)):
                part = band[row : row + size, (j - i) * NB : (j - i + 1) * NB]
                g[core_, half, x, y, start : start + size, :] = part
        if i == 0:
            pl.semaphore_wait(barrier, len(OTHERS) + GRPS - 1)
        while gone < 16 and (gone + 1) * 4 * HALF <= (packed(i, NBLK - 1) + 1) * NB:
            core_, half, x = gone // 8, gone // 4 % 2, gone % 4

            @pl.when(core != core_)
            def _():
                pair_copy(half, x).start()

            gone += 1
        fill(GAPS[0])

    def pair_sum(i):
        for h in range(2):
            a = mod4(first[h] + steps[i])
            receive(acc.at[h, a], pair_sem, (h, a))
            acc[h, a] = acc[h, a] + g[core, h, a]

    lo, hi = pl.ds(0, 2), pl.ds(2, 2)
    pair_sum(0)
    for h in range(2):
        u = first[h]
        send(acc.at[h, mod4(u + 2), lo], fwd.at[h, 0], rs_sem, (h, 0), neighbour(h, 0, 1))
        send(acc.at[h, mod4(u + 2), hi], fwd.at[h, 1], rs_sem, (h, 1), neighbour(h, 0, -1))
    pair_sum(1)
    for h in range(2):
        send(acc.at[h, mod4(first[h] + 1), hi], got.at[h, 0, hi], rs_sem, (h, 2), neighbour(h, 0, 1))
    pair_sum(2)
    for h in range(2):
        send(acc.at[h, mod4(first[h] - 1), lo], got.at[h, 1, lo], rs_sem, (h, 3), neighbour(h, 0, -1))
    pair_sum(3)
    for h in range(2):
        up, down = mod4(first[h] + 1), mod4(first[h] - 1)
        receive(fwd.at[h, 0], rs_sem, (h, 0))
        acc[h, up, 0:2] = acc[h, up, 0:2] + fwd[h, 0]
        send(acc.at[h, up, lo], got.at[h, 0, lo], rs_sem, (h, 4), neighbour(h, 0, 1))
        receive(fwd.at[h, 1], rs_sem, (h, 1))
        acc[h, down, 2:4] = acc[h, down, 2:4] + fwd[h, 1]
        send(acc.at[h, down, hi], got.at[h, 1, hi], rs_sem, (h, 5), neighbour(h, 0, -1))
    fill(GAPS[1])
    top, bottom = pl.ds(0, CUT), pl.ds(CUT, HALF - CUT)
    for h in range(2):
        u, v = first[h], second[h]
        receive(got.at[h, 0, hi], rs_sem, (h, 2))
        receive(got.at[h, 1, lo], rs_sem, (h, 3))
        receive(got.at[h, 0, lo], rs_sem, (h, 4))
        receive(got.at[h, 1, hi], rs_sem, (h, 5))
        acc[h, u] = acc[h, u] + got[h, 0] + got[h, 1]
        send(acc.at[h, u, mod4(v + 2), top], fwd_p.at[h], rs_sem, (h, 6), neighbour(h, 1, 1))
        send(acc.at[h, u, mod4(v + 2), bottom], fwd_m.at[h], rs_sem, (h, 7), neighbour(h, 1, -1))
        send(acc.at[h, u, mod4(v + 1), bottom], got2.at[h, 0, bottom], rs_sem, (h, 8), neighbour(h, 1, 1))
        send(acc.at[h, u, mod4(v - 1), top], got2.at[h, 1, top], rs_sem, (h, 9), neighbour(h, 1, -1))
    for h in range(2):
        u, up, down = first[h], mod4(second[h] + 1), mod4(second[h] - 1)
        receive(fwd_p.at[h], rs_sem, (h, 6))
        acc[h, u, up, 0:CUT] = acc[h, u, up, 0:CUT] + fwd_p[h]
        send(acc.at[h, u, up, top], got2.at[h, 0, top], rs_sem, (h, 10), neighbour(h, 1, 1))
        receive(fwd_m.at[h], rs_sem, (h, 7))
        acc[h, u, down, CUT:HALF] = acc[h, u, down, CUT:HALF] + fwd_m[h]
        send(acc.at[h, u, down, bottom], got2.at[h, 1, bottom], rs_sem, (h, 11), neighbour(h, 1, -1))
    fill(GAPS[2])
    for h in range(2):
        receive(got2.at[h, 0, bottom], rs_sem, (h, 8))
        receive(got2.at[h, 1, top], rs_sem, (h, 9))
        receive(got2.at[h, 0, top], rs_sem, (h, 10))
        receive(got2.at[h, 1, bottom], rs_sem, (h, 11))
        total = acc[h, first[h], second[h]] + got2[h, 0] + got2[h, 1]
        own[h * HALF : (h + 1) * HALF, :] = total * (1.0 / (POSITIONS * KEEP))

    def z_copy(d):
        to = lax.rem(grp + d, GRPS)
        return copy(own.at[pl.ds(z_start(to), ZROWS)], z_buf.at[d], z_sem, (d,), dev, to)

    run(1, GRPS, lambda d: z_copy(d).start())

    def block(h):
        return full.at[h, first[h], second[h], core]

    def swap(src, h):
        return copy(src.at[pl.ds(h * HALF, HALF)], block(h), swap_sem, (h,), partner)

    def spreads(i, h):
        def at(i, j):
            return full.at[h, mod4(first[h] + i), mod4(second[h] + j)]

        def both(piece, slot, dim):
            return [(piece, slot, dim, 1), (piece, slot + 1, dim, -1)]

        def on(before, after, slot, dim):
            return [(before.at[0], slot + 2, dim, 1), (after.at[1], slot + 3, dim, -1)]

        if i == 0:
            return both(at(0, 0), 0, 1) + both(at(0, 0), 4, 0)
        if i == 1:
            return on(at(0, -1), at(0, 1), 0, 1) + both(at(0, -1), 8, 0) + both(at(0, 1), 12, 0)
        if i == 2:
            return on(at(-1, 0), at(1, 0), 4, 0) + both(at(0, 2), 16, 0)
        return [x for j, slot in ((-1, 8), (1, 12), (2, 16)) for x in on(at(-1, j), at(1, j), slot, 0)]

    def needs(i, h):
        def at(i, j):
            return full.at[h, mod4(first[h] + i), mod4(second[h] + j)]

        if i == 0:
            return []
        if i == 1:
            return [(at(0, -1), 0), (at(0, 1), 1)]
        if i == 2:
            return [(at(-1, 0), 4), (at(1, 0), 5), (at(0, 2).at[0], 2), (at(0, 2).at[1], 3)]
        if i == 3:
            return [x for j, slot in ((-1, 8), (1, 12), (2, 16)) for x in ((at(-1, j), slot), (at(1, j), slot + 1))]
        return [
            x
            for j, slot in ((0, 4), (-1, 8), (1, 12), (2, 16))
            for x in ((at(2, j).at[0], slot + 2), (at(2, j).at[1], slot + 3))
        ]

    def leave(piece, slot, h, dim, step):
        return copy(piece, piece, ag_sem, (h, slot), neighbour(h, dim, step))

    def stage(i):
        for h in range(2):
            for piece, slot in needs(i, h):
                receive(piece, ag_sem, (h, slot))
            if i < 4:
                for piece, slot, dim, step in spreads(i, h):
                    leave(piece, slot, h, dim, step).start()

    def begin(src):
        for h in range(2):
            full[h, first[h], second[h], core] = src[h * HALF : (h + 1) * HALF, :]
        for h in range(2):
            receive(full.at[h, first[h], second[h], 1 - core], swap_sem, (h,))
        stage(0)

    @pl.when(core == 1)
    def _():
        for h in range(2):
            swap(own, h).start()

    fill(GAPS[3])

    @pl.when(core == 0)
    def _():
        begin(own)

    run(1, GRPS, lambda d: z_copy(d).wait())
    total = own[pl.ds(z_start(grp), ZROWS), :]
    for d in range(1, GRPS):
        total = total + z_buf[d]
    z_sum[...] = total * (1.0 / GRPS)

    def m_copy(d):
        return copy(z_sum, z_all.at[grp], m_sem, (d,), dev, lax.rem(grp + d, GRPS))

    run(1, GRPS, lambda d: m_copy(d).start())
    z_all[grp] = z_sum[...]
    fill(GAPS[4])

    @pl.when(core == 0)
    def _():
        stage(1)

    def m_receive(d):
        receive(z_all.at[lax.rem(grp + GRPS - d, GRPS)], m_sem, (d,))

    run(1, GRPS, m_receive)
    for z in range(GRPS):
        start = (z * 15) // 7 * 8
        mean[start : start + ZROWS, :] = z_all[z]

    @pl.when(core == 0)
    def _():
        for h in range(2):
            swap(mean, h).start()

    @pl.when(core == 1)
    def _():
        begin(mean)
        stage(1)

    fill(len(OTHERS))
    stage(2)
    stage(3)
    stage(4)

    run(1, GRPS, lambda d: m_copy(d).wait_send())
    for h in range(2):
        swap(own, h).wait_send()
        for i in range(4):
            for piece, slot, dim, step in spreads(i, h):
                leave(piece, slot, h, dim, step).wait_send()
    for c in sent:
        c.wait_send()
    for h in range(2):
        for a in range(4):
            pair_copy(h, a).wait_send()
    for i in range(len(OTHERS)):
        dx, dy, flip = OTHERS[i]
        copy(blocks.at[dev], arrived.at[at_offset(-dx, -dy, flip)], all_sem, (i,), partner).wait_recv()
        block_copy(i).wait_send()
    stay.wait()


def reduce_gram(kept, blocks):
    dma = pltpu.SemaphoreType.DMA
    vmem = lambda *shape: pltpu.VMEM((*shape, NB), F32)
    return pl.pallas_call(
        reduce_kernel,
        out_shape=(
            jax.ShapeDtypeStruct((2, 4, 4, 2, HALF, NB), F32),
            jax.ShapeDtypeStruct(blocks.shape, F32),
        ),
        in_specs=[pl.BlockSpec(memory_space=pltpu.HBM)] * 2,
        out_specs=(pl.BlockSpec(memory_space=pltpu.VMEM), pl.BlockSpec(memory_space=pltpu.HBM)),
        scratch_shapes=[
            pltpu.VMEM(kept.shape, F32),
            pltpu.VMEM(kept.shape, BF16),
            pltpu.VMEM(kept.shape, BF16),
            vmem(2, 2, 4, 4, HALF),
            vmem(2, 4, 4, HALF),
            vmem(2, 2, 2, HALF),
            vmem(2, 2, 4, HALF),
            vmem(2, CUT),
            vmem(2, HALF - CUT),
            vmem(2, 2, HALF),
            vmem(SHARD),
            vmem(GRPS, ZROWS),
            vmem(ZROWS),
            vmem(GRPS, ZROWS),
            vmem(SHARD),
            dma,
            dma((2, 2, 4)),
            dma((2, 2, 12)),
            dma((2, GRPS)),
            dma((2, GRPS)),
            dma((2, 2)),
            dma((2, 2, 20)),
            dma((2, len(OTHERS))),
            dma,
        ],
        compiler_params=pltpu.CompilerParams(
            collective_id=0, has_side_effects=True, vmem_limit_bytes=61 << 20
        ),
        name="reduce_gram",
    )(kept, blocks)


def diag_factor(d):
    n = NB // 8
    lane = lax.broadcasted_iota(I32, (8, NB), 1)
    sub = lax.broadcasted_iota(I32, (8, NB), 0)

    def column(x, i):
        return jnp.broadcast_to(x[:, i : i + 1], (8, NB))

    def line(x, i):
        return jnp.broadcast_to(x[i : i + 1, :], (8, NB))

    t_rows = [d[8 * s : 8 * s + 8, :] for s in range(n)]
    e_rows = [jnp.where(lane == sub + 8 * s, 1.0, 0.0).astype(F32) for s in range(n)]
    r_out, e_out = [], []
    low, scale, r_lines, e_lines = {}, [], [], []
    for s in range(n):
        c0 = 8 * s
        t, e = t_rows[s], e_rows[s]
        cols = [column(t, c0 + j) for j in range(8)]
        if s:
            before = []
            for j in range(8):
                c = column(t_rows[s], c0 - 8 + j)
                for m in range(j):
                    c = c - before[m] * low[m, j]
                before.append(c * scale[j])
            for j in range(8):
                c = before[j]
                t = t - c * r_lines[j]
                e = e - c * e_lines[j]
                cols = [x - c * line(c, k) for k, x in enumerate(cols)]
        b = {(i, j): line(cols[j], i) for i in range(8) for j in range(i, 8)}
        rows = [line(t, j) for j in range(8)]
        extra = [line(e, j) for j in range(8)]
        low, scale, r_lines, e_lines = {}, [], [], []
        r_strip = e_strip = None
        for j in range(8):
            q = lax.rsqrt(b[j, j])
            scale.append(q)
            for k in range(j + 1, 8):
                low[j, k] = b[j, k] * q
            for i in range(j + 1, 8):
                for k in range(i, 8):
                    b[i, k] = b[i, k] - low[j, i] * low[j, k]
            rj, ej = rows[j] * q, extra[j] * q
            r_lines.append(rj)
            e_lines.append(ej)
            for i in range(j + 1, 8):
                rows[i] = rows[i] - low[j, i] * rj
                extra[i] = extra[i] - low[j, i] * ej
            r_strip = rj if j == 0 else jnp.where(sub == j, rj, r_strip)
            e_strip = ej if j == 0 else jnp.where(sub == j, ej, e_strip)
        r_out.append(r_strip)
        e_out.append(e_strip)
        if s + 2 >= n:
            continue
        w = jnp.concatenate([r_strip, e_strip], axis=1)
        h = w.astype(BF16).astype(F32)
        rest = w - h
        m = rest.astype(BF16).astype(F32)
        q = rest - m
        lhs = jnp.concatenate([v[:, :NB] for v in (h, h, m, m, h, q)], axis=0).astype(BF16)
        rhs = jnp.concatenate([h, m, h, m, q, h], axis=0).astype(BF16)
        update = dot_t(lhs, rhs)
        for i in range(s + 2, n):
            t_rows[i] = t_rows[i] - update[8 * i : 8 * i + 8, :NB]
            e_rows[i] = e_rows[i] - update[8 * i : 8 * i + 8, NB:]
    return jnp.concatenate(r_out, axis=0), jnp.concatenate(e_out, axis=0)


def cholesky_kernel(g, blocks, group_rows, mean_rows, arrived, a, r, d, all_sem, stay_sem, swap_sem):
    grp = lax.axis_index("grp")
    dev = lax.axis_index("dev")
    core = lax.rem(dev, 2)
    chip = dev // 2
    cx, cy = chip // 4, lax.rem(chip, 4)

    def at_offset(dx, dy, flip):
        return (lax.rem(cx + dx + 4, 4) * 4 + lax.rem(cy + dy + 4, 4)) * 2 + lax.rem(core + flip, 2)

    def copy(src, dst, sem, at, to_dev):
        return pltpu.make_async_remote_copy(
            src_ref=src,
            dst_ref=dst,
            send_sem=sem.at[(0, *at)],
            recv_sem=sem.at[(1, *at)],
            device_id=(grp, to_dev),
            device_id_type=MESH,
        )

    barrier = pltpu.get_barrier_semaphore()
    for others in OTHERS:
        pl.semaphore_signal(barrier, inc=1, device_id=(grp, at_offset(*others)), device_id_type=MESH)

    def block_copy(i):
        to = at_offset(*OTHERS[i])
        return copy(blocks.at[to], arrived.at[dev], all_sem, (i,), to)

    stay = pltpu.make_async_copy(blocks.at[dev], arrived.at[dev], stay_sem)
    stay.start()
    pl.semaphore_wait(barrier, len(OTHERS))
    for i in range(len(OTHERS)):
        block_copy(i).start()

    for i in range(NBLK):
        for j in range(i, NBLK):
            for row, size, (core_, half, x, y), start in pieces(packed(i, j)):
                part = g[half, x, y, core_, start : start + size, :]
                a[i * NB + row : i * NB + row + size, j * NB : (j + 1) * NB] = part
    row = lax.broadcasted_iota(I32, (NB, NB), 0)
    col = lax.broadcasted_iota(I32, (NB, NB), 1)
    d[...] = a[0:NB, 0:NB]

    def step(k, c):
        top, inverse = diag_factor(d[...])
        d[...] = jnp.where(row <= col, top, 0.0)
        hi, mid = split2(inverse)
        left = jnp.concatenate([hi, hi, mid], axis=1)
        for kk in range(NBLK):

            @pl.when(k == kk)
            def _():
                k0, k1 = kk * NB, (kk + 1) * NB
                r[k0:k1, k0:k1] = d[...]
                if kk:
                    r[k0:k1, 0:k0] = jnp.zeros((NB, k0), F32)
                if kk == NBLK - 1:
                    return
                hi, mid = split2(a[k0:k1, k1:])
                strip = dot_n(left, jnp.concatenate([hi, mid, hi], axis=0))
                r[k0:k1, k1:] = strip
                hi, mid = split2(strip)
                lhs = jnp.concatenate([hi, hi, mid], axis=0)
                rhs = jnp.concatenate([hi, mid, hi], axis=0)
                d[...] = a[k1 : k1 + NB, k1 : k1 + NB] - dot_t(lhs[:, :NB], rhs[:, :NB])
                for i in range((COLS - k1) // NB):
                    lo, hi_ = i * NB, (i + 1) * NB
                    if i:
                        a[k1 + lo : k1 + hi_, k1 + lo :] -= dot_t(lhs[:, lo:hi_], rhs[:, lo:])
                    elif kk < NBLK - 2:
                        a[k1 : k1 + NB, k1 + NB :] -= dot_t(lhs[:, :NB], rhs[:, NB:])

        return c

    lax.fori_loop(0, NBLK, step, 0)

    half = COLS // DEVS
    own_rows = r.at[pl.ds(pl.multiple_of(chip * 2 * half + core * half, half), half)]
    other_rows = r.at[pl.ds(pl.multiple_of(chip * 2 * half + (1 - core) * half, half), half)]
    partner = chip * 2 + 1 - core

    @pl.when(core == 0)
    def _():
        copy(other_rows, group_rows, swap_sem, (0,), partner).start()
        group_rows[...] = own_rows[...]
        copy(other_rows, mean_rows, swap_sem, (1,), partner).wait_recv()
        copy(other_rows, group_rows, swap_sem, (0,), partner).wait_send()

    @pl.when(core == 1)
    def _():
        copy(other_rows, mean_rows, swap_sem, (1,), partner).start()
        mean_rows[...] = own_rows[...]
        copy(other_rows, group_rows, swap_sem, (0,), partner).wait_recv()
        copy(other_rows, mean_rows, swap_sem, (1,), partner).wait_send()

    for i in range(len(OTHERS)):
        dx, dy, flip = OTHERS[i]
        copy(blocks.at[dev], arrived.at[at_offset(-dx, -dy, flip)], all_sem, (i,), partner).wait_recv()
        block_copy(i).wait_send()
    stay.wait()


def cholesky_rows(full, blocks):
    vmem = pl.BlockSpec(memory_space=pltpu.VMEM)
    hbm = pl.BlockSpec(memory_space=pltpu.HBM)
    dma = pltpu.SemaphoreType.DMA
    rows = jax.ShapeDtypeStruct((COLS // DEVS, COLS), F32)
    return pl.pallas_call(
        cholesky_kernel,
        out_shape=(rows, rows, jax.ShapeDtypeStruct(blocks.shape, F32)),
        in_specs=[vmem, hbm],
        out_specs=(vmem, vmem, hbm),
        scratch_shapes=[
            pltpu.VMEM((COLS, COLS), F32),
            pltpu.VMEM((COLS, COLS), F32),
            pltpu.VMEM((NB, NB), F32),
            dma((2, len(OTHERS))),
            dma,
            dma((2, 2)),
        ],
        compiler_params=pltpu.CompilerParams(
            collective_id=1, has_side_effects=True, vmem_limit_bytes=62 << 20
        ),
        name="cholesky_rows",
    )(full, blocks)


def place_kernel(order_in, counts_in, arrived_a, arrived_b, group_in, mean_in, sketch, group_out, mean_out, order, counts, stage, zero, passed, tab_sem, row_sem, in_sem, sem):
    me = lax.axis_index("dev")
    tables = [
        pltpu.make_async_copy(order_in, order, tab_sem.at[0]),
        pltpu.make_async_copy(counts_in, counts, tab_sem.at[1]),
    ]
    for table in tables:
        table.start()
    ins = [pltpu.make_async_copy(x, passed.at[i], row_sem.at[0, i]) for i, x in enumerate((group_in, mean_in))]
    outs = [pltpu.make_async_copy(passed.at[i], x, row_sem.at[1, i]) for i, x in enumerate((group_out, mean_out))]
    for x in ins:
        x.start()
    zero[...] = jnp.zeros_like(zero)
    for table in tables:
        table.wait()

    def add(e, c):
        return c + jnp.where(e < me, counts[0, e], 0)

    offset = lax.fori_loop(0, DEVS, add, jnp.int32(0))
    held = counts[0, me]

    def load(j):
        source = order[0, jnp.minimum(offset + j, POSITIONS - 1)] >> 4
        return (
            pltpu.make_async_copy(arrived_a.at[source], stage.at[j, pl.ds(0, EARLY)], in_sem.at[j, 0]),
            pltpu.make_async_copy(arrived_b.at[source], stage.at[j, pl.ds(EARLY, KEEP - EARLY)], in_sem.at[j, 1]),
        )

    def start(j, c):
        @pl.when(j < held)
        def _():
            for part in load(j):
                part.start()

        @pl.when(j >= held)
        def _():
            pltpu.make_async_copy(zero, sketch.at[j], sem.at[j]).start()

        return c

    def store(j, c):
        @pl.when(j < held)
        def _():
            for part in load(j):
                part.wait()
            pltpu.make_async_copy(stage.at[j], sketch.at[j], sem.at[j]).start()

        return c

    def wait(j, c):
        pltpu.make_async_copy(zero, sketch.at[j], sem.at[j]).wait()
        return c

    lax.fori_loop(0, DEVS, start, 0)
    for x, y in zip(ins, outs):
        x.wait()
        y.start()
    lax.fori_loop(0, DEVS, store, 0)
    for y in outs:
        y.wait()
    lax.fori_loop(0, DEVS, wait, 0)


def place(block_order, counts, arrived_a, arrived_b, group_rows, mean_rows):
    hbm = pl.BlockSpec(memory_space=pltpu.HBM)
    return pl.pallas_call(
        place_kernel,
        out_shape=(
            jax.ShapeDtypeStruct((DEVS, KEEP, COLS), F32),
            jax.ShapeDtypeStruct(group_rows.shape, F32),
            jax.ShapeDtypeStruct(mean_rows.shape, F32),
        ),
        in_specs=[hbm] * 6,
        out_specs=(hbm, hbm, hbm),
        scratch_shapes=[
            pltpu.SMEM((1, POSITIONS), I32),
            pltpu.SMEM((1, DEVS), I32),
            pltpu.VMEM((DEVS, KEEP, COLS), F32),
            pltpu.VMEM((KEEP, COLS), F32),
            pltpu.VMEM((2, COLS // DEVS, COLS), F32),
            pltpu.SemaphoreType.DMA((2,)),
            pltpu.SemaphoreType.DMA((2, 2)),
            pltpu.SemaphoreType.DMA((DEVS, 2)),
            pltpu.SemaphoreType.DMA((DEVS,)),
        ],
        compiler_params=pltpu.CompilerParams(vmem_limit_bytes=62 << 20),
        name="place_slots",
    )(block_order, counts, arrived_a, arrived_b, group_rows, mean_rows)


def body(matrix, block_order, counts, sign_bits, row_mask):
    early, late, kept = mix(matrix, block_order, counts, sign_bits, row_mask)
    full, early = reduce_gram(kept, early)
    group_rows, mean_rows, late = cholesky_rows(full, late)
    sketch, group_rows, mean_rows = place(block_order, counts, early, late, group_rows, mean_rows)
    return sketch.reshape(DEVS * KEEP, COLS), group_rows[None], mean_rows


def solution(mesh):
    placed = (
        P(("grp", "dev"), None),
        P("grp", None),
        P("grp", None),
        P("grp", None, None),
        P("grp", None, None),
    )
    return jax.shard_map(
        body,
        mesh=mesh,
        in_specs=placed,
        out_specs=(P(("grp", "dev"), None), P("grp", "dev", None), P("dev", None)),
        check_vma=False,
    )
```
